32 devices in a mesh: blk: 8 (over z, y), circ: 4 (over x, core).
Axes of the slice: x: 2, y: 2, z: 4, core: 2. Of those that a mesh axis runs over, the one named last changes fastest.
Arguments:
- panels: float32 [4, 1024], P(None, ('blk', 'circ')), may hold values from -2 to 2, as said below
- node_of_panel: int32 [1024], P(('blk', 'circ')), may hold values from 0 to 2047, as said below
- stiffener_rows: int32 [4], replicated, may hold values from 0 to 63
- density_start: float32 [16, 1024], P(None, ('blk', 'circ')), may hold values from -6 to 6
- motion_start: float32 [16, 64, 1024], P(None, 'blk', 'circ'), may hold values from -6 to 6
- force: float32 [16, 64, 1024], P(None, 'blk', 'circ'), may hold values from -128 to 128
- stiffness: float32 [64, 1024], P('blk', 'circ'), may hold values from 0.5 to 2
Outputs:
- source_density: float32 [16, 1024], P(None, ('blk', 'circ'))
- surface_pressure: float32 [16, 1024], P(None, ('blk', 'circ'))
- shell_motion: float32 [16, 64, 1024], P(None, 'blk', 'circ')
The draws below stay inside these ranges and needn't reach their ends.
Inputs may be any that keep to these rules, and one draw needn't show every extreme that they name: `panels`: every panel lies between 0.98 and 1.02 from the z axis, with z between -2 and 2 and area between 0.5 and 2 times 8 pi / 1024. `node_of_panel`: counted as row * 256 + column within the tile of the device that holds the panel. `stiffener_rows`: A row may be listed more than once.
All inputs are finite; a program needn't handle non-finite values.
Results may differ from the reference program's by a relative error of at most 0.0029.
Values may be sent and summed in bfloat16 or wider, within the bound.
A program may use at most 64 MiB of HBM per device.

```python
import math
import jax
import jax.numpy as jnp
from jax import lax

PD = 32
SA = 8
SC = 256
LOADS = 8
ITERS = 4
SWEEPS = 2
PANELS = 1024
NA = 64
NC = 1024
HOOPS = 4
N_CIRC = 4


def panel_nodes(key):
    return jax.random.randint(jax.random.fold_in(key, 11), (PANELS,), 0, SA * SC, dtype=jnp.int32)


def draw_node_of_panel(key, part):
    return panel_nodes(key)


def draw_panels(key, part):
    nodes = panel_nodes(key)
    device_of = jnp.arange(PANELS, dtype=jnp.int32) // PD
    circ_count = NC // SC
    node_row = device_of // circ_count * SA + nodes // SC
    node_col = device_of % circ_count * SC + nodes % SC
    keys = jax.random.split(jax.random.fold_in(key, 23), 4)
    axial_jitter = jax.random.uniform(keys[0], (PANELS,), jnp.float32)
    angle_jitter = jax.random.uniform(keys[1], (PANELS,), jnp.float32)
    radial_jitter = 2.0 * jax.random.uniform(keys[2], (PANELS,), jnp.float32) - 1.0
    area_jitter = jax.random.uniform(keys[3], (PANELS,), jnp.float32)
    height = (node_row.astype(jnp.float32) + axial_jitter) * (4.0 / NA) - 2.0
    angle = (node_col.astype(jnp.float32) + angle_jitter) * (2.0 * math.pi / NC)
    radius = 1.0 + 0.02 * radial_jitter
    areas = 8.0 * math.pi / PANELS * jnp.exp(math.log(0.5) + math.log(4.0) * area_jitter)
    return jnp.stack([radius * jnp.cos(angle), radius * jnp.sin(angle), height, areas], axis=0)


def place_ends(array, key, low, high):
    shape = array.shape
    index_at = [jax.random.randint(jax.random.fold_in(key, axis), (), 0, shape[axis]) for axis in range(len(shape))]
    array = array.at[tuple(index_at)].set(low)
    longest = shape.index(max(shape))
    index_at[longest] = (index_at[longest] + 1) % shape[longest]
    return array.at[tuple(index_at)].set(high)


def block_levels(key, shape, shards, least, top_value):
    def one(position, blocks):
        heights = jax.random.uniform(jax.random.fold_in(jax.random.fold_in(key, 6), position), (blocks,), jnp.float32, least / len(shards), top_value / len(shards))
        return jnp.repeat(jnp.exp(heights), shape[position] // blocks).reshape((-1,) + (1,) * (len(shape) - position - 1))

    factor_of = one(*shards[0])
    for cut in shards[1:]:
        factor_of = factor_of * one(*cut)
    return factor_of


def centred(rng, dims, deviation, bound, shards=(), held_as=jnp.bfloat16):
    values = jax.random.normal(rng, dims, jnp.float32) * deviation
    if len(shards) > 0:
        values = block_levels(rng, dims, shards, -0.22, 0.18) * values
    return jnp.clip(values, min=-bound, max=bound).astype(held_as)


def setup_inputs(seed: int = 0) -> dict:
    streams_of = jax.random.split(jax.random.key(seed), 8)
    panels = draw_panels(jax.random.fold_in(streams_of[7], 71), 0)
    node_of_panel = draw_node_of_panel(jax.random.fold_in(streams_of[7], 71), 0)
    stiffener_rows = place_ends(jax.random.randint(streams_of[2], (HOOPS,), 0, NA), jax.random.fold_in(streams_of[2], 1), 0, NA - 1).astype(jnp.int32)
    density_start = centred(streams_of[3], (2 * LOADS, PANELS), 1.0, 6.0, ((1, 32),), jnp.float32)
    motion_start = centred(streams_of[4], (2 * LOADS, NA, NC), 1.0, 6.0, ((1, 8), (2, 4)), jnp.float32)
    force = centred(streams_of[5], (2 * LOADS, NA, NC), 20.0, 128.0, ((1, 8), (2, 4)), jnp.float32)
    stiffness = jnp.clip(jnp.exp(math.log(2.0) - 1.3862944 * jax.random.uniform(streams_of[6], (NA, NC), jnp.float32) ** block_levels(streams_of[6], (NA, NC), ((0, 8), (1, 4)), -0.2, 0.2)), 0.5, 2.0)
    return {"panels": panels, "node_of_panel": node_of_panel, "stiffener_rows": stiffener_rows, "density_start": density_start, "motion_start": motion_start, "force": force, "stiffness": stiffness}


wave_number = 4.0
single_scale = 30.0
double_scale = 6.0
hoop_spring = 40.0
inertia_term = 4.0
loss_factor = 0.2
relaxation = 0.3

def kernel_blocks(targets, sources):
    radial = jnp.sqrt(targets[0] * targets[0] + targets[1] * targets[1])
    normal_x = (targets[0] / radial)[:, None]
    normal_y = (targets[1] / radial)[:, None]
    delta_x = targets[0][:, None] - sources[0][None, :]
    delta_y = targets[1][:, None] - sources[1][None, :]
    delta_z = targets[2][:, None] - sources[2][None, :]
    areas = sources[3][None, :]
    dist_sq = delta_x * delta_x + delta_y * delta_y + delta_z * delta_z + areas / math.pi
    distance = jnp.sqrt(dist_sq)
    inverse = 1.0 / distance
    phase_arg = wave_number * distance
    cosine = jnp.cos(phase_arg)
    sine_part = jnp.sin(phase_arg)
    weight = areas * (1.0 / (4.0 * math.pi)) * inverse
    single = single_scale * weight
    double = double_scale * weight * (normal_x * delta_x + normal_y * delta_y) * inverse * inverse
    real_stack = jnp.concatenate([single * cosine, double * (-cosine - phase_arg * sine_part)], axis=0)
    imag_stack = jnp.concatenate([single * sine_part, double * (phase_arg * cosine - sine_part)], axis=0)
    return (real_stack.astype(jnp.bfloat16), imag_stack.astype(jnp.bfloat16))

def laplace_full(field):
    widths = [(0, 0)] * (field.ndim - 2) + [(1, 1), (0, 0)]
    padded = jnp.pad(field, widths)
    return padded[..., 2:, :] + padded[..., :-2, :] + jnp.roll(field, 1, axis=-1) + jnp.roll(field, -1, axis=-1) - 4.0 * field

def relax(motion, bend, load, stiffness, hoop_rows):
    half = motion.shape[0] // 2
    shift = hoop_spring * hoop_rows - inertia_term
    applied_re = bend[:half] - loss_factor * bend[half:] + shift * motion[:half]
    applied_im = bend[half:] + loss_factor * bend[:half] + shift * motion[half:]
    resid_re = load[:half] - applied_re
    resid_im = load[half:] - applied_im
    diag_re = 20.0 * stiffness + shift
    diag_im = 20.0 * loss_factor * stiffness
    denom = diag_re * diag_re + diag_im * diag_im
    update_re = (resid_re * diag_re + resid_im * diag_im) / denom
    update_im = (resid_im * diag_re - resid_re * diag_im) / denom
    return motion + relaxation * jnp.concatenate([update_re, update_im], axis=0)

def reference(panels, node_of_panel, stiffener_rows, density_start, motion_start, force, stiffness):
    panel_count = panels.shape[1]
    channels = density_start.shape[0]
    half = channels // 2
    axial_rows = motion_start.shape[1]
    columns = motion_start.shape[2]
    device_of = jnp.arange(panel_count, dtype=jnp.int32) // PD
    blk_of = device_of // N_CIRC
    circ_of = device_of % N_CIRC
    node_row = blk_of * SA + node_of_panel // SC
    node_col = circ_of * SC + node_of_panel % SC
    node_flat = (node_row * columns + node_col).astype(jnp.int32)
    hoop_rows = jnp.any(jnp.arange(axial_rows, dtype=jnp.int32)[:, None] == stiffener_rows[None, :], axis=1)
    hoop_rows = hoop_rows.astype(jnp.float32)[:, None]
    panel_weight = panels[3] * (panel_count / (8.0 * math.pi))
    row_block = math.gcd(panel_count, 256)
    block_count = panel_count // row_block
    target_blocks = jnp.transpose(panels.reshape(4, block_count, row_block), (1, 0, 2))
    density = density_start
    motion = motion_start
    pressure = jnp.zeros_like(density_start)
    for round_index in range(ITERS):
        neumann = motion.reshape(channels, axial_rows * columns)[:, node_flat]
        density_bf = lax.optimization_barrier(density.astype(jnp.bfloat16)).astype(jnp.float32)
        rotated = jnp.concatenate([-density_bf[half:], density_bf[:half]], axis=0)

        def apply_rows(target_block):
            real_stack, imag_stack = kernel_blocks(target_block, panels)
            real_f = lax.optimization_barrier(real_stack).astype(jnp.float32)
            imag_f = lax.optimization_barrier(imag_stack).astype(jnp.float32)
            first = jnp.einsum('lc,rc->lr', density_bf, real_f, precision=lax.Precision.HIGHEST)
            second = jnp.einsum('lc,rc->lr', rotated, imag_f, precision=lax.Precision.HIGHEST)
            return first + second
        results = lax.map(apply_rows, target_blocks)
        single_part = jnp.transpose(results[:, :, :row_block], (1, 0, 2)).reshape(channels, panel_count)
        double_part = jnp.transpose(results[:, :, row_block:], (1, 0, 2)).reshape(channels, panel_count)
        pressure = single_part
        density = 0.5 * density + neumann - double_part
        fluid = jnp.zeros((channels, axial_rows * columns), jnp.float32)
        fluid = fluid.at[:, node_flat].add(panel_weight[None, :] * pressure)
        load = force - fluid.reshape(channels, axial_rows, columns)
        for sweep_index in range(SWEEPS):
            bend = laplace_full(stiffness * laplace_full(motion))
            motion = relax(motion, bend, load, stiffness, hoop_rows)
    return (density, pressure, motion)
```

```python
import functools
import math

import jax
import jax.numpy as jnp
from jax import lax
from jax.experimental import pallas as pl
from jax.experimental.pallas import tpu as pltpu
from jax.sharding import PartitionSpec as P

MESH = pl.DeviceIdType.MESH
ITERS = 4
SWEEPS = 2
STEPS = ITERS * SWEEPS

wave_number = 4.0
single_scale = 30.0
double_scale = 6.0
hoop_spring = 40.0
inertia_term = 4.0
loss_factor = 0.2
relaxation = 0.3

COS = (
    0.9999999890590228, -19.739204499454, 64.93911745989914, -85.45013953093448,
    60.16763095128989, -25.96759924954187, 6.528658162606979,
)
SIN = (
    6.283185302511502, -41.34170040531754, 81.6051313857969, -76.70301535383193,
    42.02592698564183, -14.899846667160109, 3.2381375090822355,
)

UP, DOWN, LEFT, RIGHT, UL, UR, DL, DR = range(8)
OPPOSITE = {UP: DOWN, DOWN: UP, LEFT: RIGHT, RIGHT: LEFT, UL: DR, UR: DL, DL: UR, DR: UL}


def poly(coefs, x):
    acc = jnp.full_like(x, coefs[-1])
    for c in coefs[-2::-1]:
        acc = acc * x + c
    return acc


def split(x):
    high = x.astype(jnp.bfloat16)
    low = (x - high.astype(jnp.float32)).astype(jnp.bfloat16)
    return high, low


def dot(a, b, dims):
    return lax.dot_general(a, b, (dims, ((), ())), preferred_element_type=jnp.float32)


def kernel(
    nb, nc, pd,
    panels, node, hoops, density_in, motion_in, force_in, stiff,
    density_out, pressure_out, motion_out,
    mot, frc, rows_in, cols_in, cols_own, stiff_in, kext, coef, onehot, rowhot,
    dens, press, wide, ga, gb, ga_src, pa, pb, pa_src, mats,
    sh_send, sh_recv, st_send, st_recv, a_send, a_recv, b_send, b_recv, pan_send, pan_recv,
):
    f32 = jnp.float32
    b = lax.axis_index("blk")
    c = lax.axis_index("circ")
    axial, circum = stiff.shape
    last_tile = circum - 128
    cleft, cright = lax.rem(c + nc - 1, nc), lax.rem(c + 1, nc)
    where_to = {
        UP: (b - 1, c), DOWN: (b + 1, c), LEFT: (b, cleft), RIGHT: (b, cright),
        UL: (b - 1, cleft), UR: (b - 1, cright), DL: (b + 1, cleft), DR: (b + 1, cright),
    }
    has_up, has_down = b > 0, b < nb - 1

    def for_dirs(fn):
        fn(LEFT)
        fn(RIGHT)

        @pl.when(has_up)
        def _():
            for d in (UP, UL, UR):
                fn(d)

        @pl.when(has_down)
        def _():
            for d in (DOWN, DL, DR):
                fn(d)

    def for_peers(fn):
        if nb <= 8:
            for j in range(1, nb):
                fn(lax.rem(b + j, nb))
        else:
            def body(j, _):
                fn(lax.rem(b + j, nb))
                return 0

            lax.fori_loop(1, nb, body, 0)

    @pl.when(jnp.logical_not(has_up))
    def _():
        rows_in[:, 0] = jnp.zeros_like(rows_in[:, 0])
        cols_in[:, UL - 2] = jnp.zeros_like(cols_in[:, UL - 2])
        cols_in[:, UR - 2] = jnp.zeros_like(cols_in[:, UR - 2])
        stiff_in[UP] = jnp.zeros_like(stiff_in[UP])

    @pl.when(jnp.logical_not(has_down))
    def _():
        rows_in[:, 1] = jnp.zeros_like(rows_in[:, 1])
        cols_in[:, DL - 2] = jnp.zeros_like(cols_in[:, DL - 2])
        cols_in[:, DR - 2] = jnp.zeros_like(cols_in[:, DR - 2])
        stiff_in[DOWN] = jnp.zeros_like(stiff_in[DOWN])

    barrier = pltpu.get_barrier_semaphore()

    def greet(device):
        pl.semaphore_signal(barrier, inc=1, device_id=device, device_id_type=MESH)

    for j in range(1, nc):
        greet((b, lax.rem(c + j, nc)))
    for_peers(lambda peer: greet((peer, c)))

    @pl.when(has_up)
    def _():
        greet(where_to[UL])
        greet(where_to[UR])

    @pl.when(has_down)
    def _():
        greet(where_to[DL])
        greet(where_to[DR])

    lane = lax.broadcasted_iota(jnp.int32, (16, 128), 1)
    lane8 = lane[:8]

    def spread(x):
        x = jnp.where(lane[: x.shape[0]] < pd, x, 0.0)
        step = pd
        while step < 128:
            x = x + pltpu.roll(x, step, 1)
            step *= 2
        return x

    wide[...] = jnp.zeros_like(wide)
    wide[0:4, 0:pd] = panels[...]
    wide[8:24, 0:pd] = density_in[...]
    own = spread(wide[0:8, :])
    dens[...] = spread(wide[8:24, :])
    pa_src[...] = own
    ga_src[0] = dens[...].astype(jnp.bfloat16)

    pl.semaphore_wait(
        barrier,
        (nc - 1) + (nb - 1) + 2 * has_up.astype(jnp.int32) + 2 * has_down.astype(jnp.int32),
    )

    def copy(src, dst, send, recv, device):
        return pltpu.make_async_remote_copy(
            src_ref=src, dst_ref=dst, send_sem=send, recv_sem=recv,
            device_id=device, device_id_type=MESH,
        )

    me = (b, c)

    def a_start(rnd):
        for j in range(1, nc):
            copy(ga_src.at[rnd], ga.at[rnd, j - 1], a_send.at[rnd, j - 1], a_recv.at[rnd, j - 1],
                 (b, lax.rem(c + j, nc))).start()

    def a_wait(rnd):
        for j in range(1, nc):
            copy(ga_src.at[rnd], ga.at[rnd, j - 1], a_send.at[rnd, j - 1], a_recv.at[rnd, j - 1],
                 me).wait_recv()

    def merge(own_block, parts):
        group = lane[: own_block.shape[0]] // pd
        out = own_block
        for j in range(1, nc):
            out = jnp.where(group == lax.rem(c + nc - j, nc), parts[j - 1], out)
        return out

    def b_start(rnd):
        parts = [ga[rnd, j].astype(f32) for j in range(nc - 1)]
        gb[rnd, b] = merge(ga_src[rnd].astype(f32), parts).astype(jnp.bfloat16)
        for_peers(lambda peer: copy(gb.at[rnd, b], gb.at[rnd, b], b_send.at[rnd], b_recv.at[rnd],
                                    (peer, c)).start())

    def b_all(rnd):
        part = gb.at[rnd, pl.ds(0, nb - 1)]
        return copy(part, part, b_send.at[rnd], b_recv.at[rnd], me)

    for j in range(1, nc):
        copy(pa_src, pa.at[j - 1], pan_send.at[j - 1], pan_recv.at[j - 1],
             (b, lax.rem(c + j, nc))).start()
    a_start(0)
    stiff_dirs = (UP, DOWN, LEFT, RIGHT)

    def stiff_copy(d):
        return copy(stiff, stiff_in.at[OPPOSITE[d]], st_send.at[d], st_recv.at[OPPOSITE[d]],
                    where_to[d])

    for_dirs(lambda d: stiff_copy(d).start() if d in stiff_dirs else None)

    def shell_copy(s, d):
        o = OPPOSITE[d]
        if d in (UP, DOWN):
            src = mot.at[s, pl.ds(0 if d == UP else axial - 2, 2)]
            dst = rows_in.at[s, 0 if o == UP else 1]
        else:
            src, dst = cols_own.at[s], cols_in.at[s, o - 2]
        return copy(src, dst, sh_send.at[s, d], sh_recv.at[s, o], where_to[d])

    def shell_recv(s, d):
        if d in (UP, DOWN):
            dst = rows_in.at[s, 0 if d == UP else 1]
        else:
            dst = cols_in.at[s, d - 2]
        return copy(dst, dst, sh_send.at[s, d], sh_recv.at[s, d], me)

    place = (lane + 2) & 127
    row_of = ((128 - (place - (place & 3))) & 127) // 4

    def shell_start(s, rows):
        packed = None
        for r in range(axial):
            edge = jnp.where(lane < 64, rows[r][:, :128], rows[r][:, last_tile:])
            edge = pltpu.roll(edge, (128 - 4 * r) % 128, 1) if r else edge
            packed = edge if r == 0 else jnp.where(row_of == r, edge, packed)
        cols_own[s] = packed
        for_dirs(lambda d: shell_copy(s, d).start())

    first = []
    for r in range(axial):
        row = motion_in[:, r, :]
        mot[0, r] = row
        first.append(row)
    shell_start(0, first)
    for r in range(axial):
        frc[r] = force_in[:, r, :]

    sub = lax.broadcasted_iota(jnp.int32, (axial, circum), 0) + b * axial
    hoop = jnp.zeros((axial, circum), f32)
    for h in range(hoops.shape[0]):
        hoop = jnp.where(sub == hoops[h], 1.0, hoop)
    k = stiff[...]
    shift = hoop_spring * hoop - inertia_term
    diag_re = 20.0 * k + shift
    diag_im = (20.0 * loss_factor) * k
    scale = relaxation / (diag_re * diag_re + diag_im * diag_im)
    inv_re, inv_im = diag_re * scale, diag_im * scale
    for r in range(axial):
        for n, x in enumerate((shift, inv_re, inv_im)):
            coef[n, r] = jnp.broadcast_to(x[r : r + 1], (8, circum))

    nodes = jnp.zeros((8, 128), jnp.int32)
    for p in range(pd):
        nodes = jnp.where((lane8 & (pd - 1)) == p, node[p], nodes)
    node_row = nodes // circum
    node_col = nodes - node_row * circum
    rowhot[...] = (node_row == lax.broadcasted_iota(jnp.int32, (8, 128), 0)).astype(f32)
    col_iota = lax.broadcasted_iota(jnp.int32, (circum, 128), 0)
    onehot[...] = (
        (jnp.broadcast_to(node_col[0:1], (circum, 128)) == col_iota).astype(f32).astype(jnp.bfloat16)
    )

    for j in range(1, nc):
        copy(pa_src, pa.at[j - 1], pan_send.at[j - 1], pan_recv.at[j - 1], me).wait_recv()
    a_wait(0)
    pb[b] = merge(pa_src[...], [pa[j] for j in range(nc - 1)])
    for_peers(lambda peer: copy(pb.at[b], pb.at[b], pan_send.at[nc - 1], pan_recv.at[nc - 1],
                                (peer, c)).start())
    b_start(0)
    pb_part = pb.at[pl.ds(0, nb - 1)]
    pb_all = copy(pb_part, pb_part, pan_send.at[nc - 1], pan_recv.at[nc - 1], me)

    for_dirs(
        lambda d: copy(stiff_in.at[d], stiff_in.at[d], st_send.at[d], st_recv.at[d], me).wait_recv()
        if d in stiff_dirs else None
    )
    right_tile = stiff_in[RIGHT][:, :128]
    left_tile = stiff_in[LEFT][:, last_tile:]
    side = jnp.where(lane8 < 64, right_tile, left_tile)
    k_up, k_down = stiff_in[UP], stiff_in[DOWN]
    for r in range(axial + 2):
        if r == 0:
            line = k_up[axial - 1 : axial]
        elif r == axial + 1:
            line = k_down[0:1]
        else:
            line = k[r - 1 : r]
            kext[r, :, circum:] = jnp.broadcast_to(side[r - 1 : r], (16, 128))
        kext[r, :, :circum] = jnp.broadcast_to(line, (16, circum))

    radial = jnp.sqrt(own[0:1] * own[0:1] + own[1:2] * own[1:2])
    eye = lax.broadcasted_iota(jnp.int32, (pd, 128), 0) == lax.broadcasted_iota(
        jnp.int32, (pd, 128), 1
    )

    def column(line):
        return jnp.sum(jnp.where(eye, jnp.broadcast_to(line, (pd, 128)), 0.0), axis=1, keepdims=True)

    tx, ty, tz = column(own[0:1]), column(own[1:2]), column(own[2:3])
    nx, ny = column(own[0:1] / radial), column(own[1:2] / radial)
    weight_row = own[3:4] * (pd * nb * nc / (8.0 * math.pi))

    pb_all.wait_recv()

    per = mats.shape[2] // 128
    for q in range(nb // per):
        for i in range(per):
            src = pb[q * per + i]
            dx, dy, dz = tx - src[0:1], ty - src[1:2], tz - src[2:3]
            area = src[3:4]
            dist_sq = dx * dx + dy * dy + dz * dz + area * (1.0 / math.pi)
            inverse = lax.rsqrt(dist_sq)
            phase = (wave_number * dist_sq) * inverse
            turns = phase * (1.0 / (2.0 * math.pi))
            turns = turns - jnp.round(turns)
            sq = turns * turns
            cosine = poly(COS, sq)
            sine = poly(SIN, sq) * turns
            weight = area * (1.0 / (4.0 * math.pi)) * inverse
            single = single_scale * weight
            double = double_scale * weight * (nx * dx + ny * dy) * inverse * inverse
            at = pl.ds(i * 128, 128)
            bf = jnp.bfloat16
            mats[q, 0:pd, at] = (single * cosine).astype(bf)
            mats[q, pd : 2 * pd, at] = (double * (-cosine - phase * sine)).astype(bf)
            mats[q, 2 * pd : 3 * pd, at] = (single * sine).astype(bf)
            mats[q, 3 * pd : 4 * pd, at] = (double * (phase * cosine - sine)).astype(bf)

    left_lanes = (lane & 3) >= 2

    def sweep(s):
        for_dirs(lambda d: shell_recv(s, d).wait_recv())
        tile = lambda d: cols_in[s, d - 2]
        side_own = jnp.where(left_lanes, tile(LEFT), tile(RIGHT))
        side_up = jnp.where(left_lanes, tile(UL), tile(UR))
        side_down = jnp.where(left_lanes, tile(DL), tile(DR))
        v = {}
        for r in range(axial):
            edge = pltpu.roll(side_own, 4 * r, 1) if r else side_own
            v[r] = jnp.concatenate([mot[s, r], edge], axis=1)
        v[-1] = jnp.concatenate([rows_in[s, 0, 1], pltpu.roll(side_up, 4 * (axial - 1), 1)], axis=1)
        v[axial] = jnp.concatenate([rows_in[s, 1, 0], side_down], axis=1)
        width = circum + 128

        def across(x):
            return pltpu.roll(x, 1, 1) + pltpu.roll(x, width - 1, 1) - 4.0 * x

        moment = {}
        for r in range(-1, axial + 1):
            if r == -1:
                lap = across(v[r])[:, :circum] + rows_in[s, 0, 0] + v[0][:, :circum]
            elif r == axial:
                lap = across(v[r])[:, :circum] + rows_in[s, 1, 1] + v[axial - 1][:, :circum]
            else:
                lap = across(v[r]) + v[r - 1] + v[r + 1]
            moment[r] = kext[r + 1, :, : lap.shape[1]] * lap
        out = []
        for r in range(axial):
            bend = (
                across(moment[r])[:, :circum]
                + moment[r - 1][:, :circum]
                + moment[r + 1][:, :circum]
            )
            here, load = mot[s, r], frc[axial + r]
            bend_re, bend_im = bend[:8], bend[8:]
            v_re, v_im = here[:8], here[8:]
            sh, a, m = coef[0, r], coef[1, r], coef[2, r]
            res_re = load[:8] - (bend_re - loss_factor * bend_im + sh * v_re)
            res_im = load[8:] - (bend_im + loss_factor * bend_re + sh * v_im)
            new = jnp.concatenate(
                [v_re + res_re * a + res_im * m, v_im + res_im * a - res_re * m], axis=0
            )
            mot[s + 1, r] = new
            out.append(new)
        return out

    def round_body(rnd, _):
        b_all(rnd).wait_recv()
        total = None
        for q in range(nb // per):
            block = jnp.concatenate([gb[rnd, q * per + i] for i in range(per)], axis=1)
            term = dot(block, mats[q], ((1,), (1,)))
            total = term if total is None else total + term
        re, im = total[:8], total[8:]
        both = jnp.concatenate(
            [re - pltpu.roll(im, 2 * pd, 1), im + pltpu.roll(re, 2 * pd, 1)], axis=0
        )
        pressure = spread(both)
        press[...] = pressure
        double = spread(pltpu.roll(both, 128 - pd, 1))
        s = SWEEPS * rnd
        neumann = jnp.zeros((16, 128), f32)
        picked = None
        for part in split(mot[s].reshape(axial * 16, circum)):
            term = dot(part, onehot[...], ((1,), (0,)))
            picked = term if picked is None else picked + term
        picked = picked.reshape(axial, 16, 128)
        for r in range(axial):
            neumann = neumann + picked[r] * rowhot[r : r + 1]
        density = 0.5 * dens[...] + neumann - double
        dens[...] = density

        @pl.when(rnd < ITERS - 1)
        def _():
            ga_src[rnd + 1] = density.astype(jnp.bfloat16)
            a_start(rnd + 1)

        weighted = jnp.where(lane < pd, pressure * weight_row, 0.0)
        spots = jnp.concatenate([weighted * rowhot[r : r + 1] for r in range(axial)], axis=0)
        fluid = None
        for part in split(spots):
            term = dot(part, onehot[...], ((1,), (1,)))
            fluid = term if fluid is None else fluid + term
        fluid = fluid.reshape(axial, 16, circum)
        for r in range(axial):
            frc[axial + r] = frc[r] - fluid[r]

        for i in range(SWEEPS):
            rows = sweep(s + i)
            if i < SWEEPS - 1:
                shell_start(s + i + 1, rows)

                @pl.when(rnd < ITERS - 1)
                def _():
                    a_wait(rnd + 1)
                    b_start(rnd + 1)
            else:
                @pl.when(rnd < ITERS - 1)
                def _():
                    shell_start(s + i + 1, rows)
        return 0

    lax.fori_loop(0, ITERS, round_body, 0)

    density_out[...] = dens[...][:, :pd]
    pressure_out[...] = press[...][:, :pd]
    for r in range(axial):
        motion_out[:, r, :] = mot[STEPS, r]

    for j in range(1, nc):
        copy(pa_src, pa.at[j - 1], pan_send.at[j - 1], pan_recv.at[j - 1], me).wait_send()
    pb_all.wait_send()
    for_dirs(lambda d: stiff_copy(d).wait_send() if d in stiff_dirs else None)

    def finish_round(rnd, _):
        for j in range(1, nc):
            copy(ga_src.at[rnd], ga.at[rnd, j - 1], a_send.at[rnd, j - 1], a_recv.at[rnd, j - 1],
                 me).wait_send()
        b_all(rnd).wait_send()
        for i in range(SWEEPS):
            for_dirs(lambda d: shell_copy(SWEEPS * rnd + i, d).wait_send())
        return 0

    lax.fori_loop(0, ITERS, finish_round, 0)


def per_device(nb, nc, panels, node, hoops, density, motion, force, stiffness):
    pd = panels.shape[1]
    channels, axial, circum = motion.shape
    per = math.gcd(nb, 8)
    f32, bf16 = jnp.float32, jnp.bfloat16
    vmem = pl.BlockSpec(memory_space=pltpu.VMEM)
    smem = pl.BlockSpec(memory_space=pltpu.SMEM)
    dma = pltpu.SemaphoreType.DMA
    scratch = [
        pltpu.VMEM((STEPS + 1, axial, channels, circum), f32),
        pltpu.VMEM((2 * axial, channels, circum), f32),
        pltpu.VMEM((STEPS, 2, 2, channels, circum), f32),
        pltpu.VMEM((STEPS, 6, channels, 128), f32),
        pltpu.VMEM((STEPS, channels, 128), f32),
        pltpu.VMEM((4, axial, circum), f32),
        pltpu.VMEM((axial + 2, channels, circum + 128), f32),
        pltpu.VMEM((3, axial, 8, circum), f32),
        pltpu.VMEM((circum, 128), bf16),
        pltpu.VMEM((8, 128), f32),
        pltpu.VMEM((channels, 128), f32),
        pltpu.VMEM((channels, 128), f32),
        pltpu.VMEM((24, 128), f32),
        pltpu.VMEM((ITERS, nc - 1, channels, 128), bf16),
        pltpu.VMEM((ITERS, nb, channels, 128), bf16),
        pltpu.VMEM((ITERS, channels, 128), bf16),
        pltpu.VMEM((nc - 1, 8, 128), f32),
        pltpu.VMEM((nb, 8, 128), f32),
        pltpu.VMEM((8, 128), f32),
        pltpu.VMEM((nb // per, 4 * pd, per * 128), bf16),
        dma((STEPS, 8)), dma((STEPS, 8)), dma((4,)), dma((4,)),
        dma((ITERS, nc - 1)), dma((ITERS, nc - 1)), dma((ITERS,)), dma((ITERS,)),
        dma((nc,)), dma((nc,)),
    ]
    return pl.pallas_call(
        functools.partial(kernel, nb, nc, pd),
        out_shape=(
            jax.ShapeDtypeStruct(density.shape, f32),
            jax.ShapeDtypeStruct(density.shape, f32),
            jax.ShapeDtypeStruct(motion.shape, f32),
        ),
        in_specs=[vmem, smem, smem, vmem, vmem, vmem, vmem],
        out_specs=(vmem, vmem, vmem),
        scratch_shapes=scratch,
        compiler_params=pltpu.CompilerParams(
            collective_id=0, has_side_effects=True, vmem_limit_bytes=40 * 1024 * 1024
        ),
    )(panels, node, hoops, density, motion, force, stiffness)


def solution(mesh):
    nb, nc = mesh.shape["blk"], mesh.shape["circ"]
    in_specs = (
        P(None, ("blk", "circ")),
        P(("blk", "circ")),
        P(),
        P(None, ("blk", "circ")),
        P(None, "blk", "circ"),
        P(None, "blk", "circ"),
        P("blk", "circ"),
    )
    out_specs = (P(None, ("blk", "circ")), P(None, ("blk", "circ")), P(None, "blk", "circ"))
    return jax.shard_map(
        functools.partial(per_device, nb, nc),
        mesh=mesh, in_specs=in_specs, out_specs=out_specs, check_vma=False,
    )
```

```python
import functools
import math

import jax
import jax.numpy as jnp
from jax import lax
from jax.experimental import pallas as pl
from jax.experimental.pallas import tpu as pltpu
from jax.sharding import PartitionSpec as P

MESH = pl.DeviceIdType.MESH
ITERS = 4
SWEEPS = 2
STEPS = ITERS * SWEEPS

wave_number = 4.0
single_scale = 30.0
double_scale = 6.0
hoop_spring = 40.0
inertia_term = 4.0
loss_factor = 0.2
relaxation = 0.3

COS = (
    0.9999999890590228, -19.739204499454, 64.93911745989914, -85.45013953093448,
    60.16763095128989, -25.96759924954187, 6.528658162606979,
)
SIN = (
    6.283185302511502, -41.34170040531754, 81.6051313857969, -76.70301535383193,
    42.02592698564183, -14.899846667160109, 3.2381375090822355,
)

UP, DOWN, LEFT, RIGHT, UL, UR, DL, DR = range(8)
OPPOSITE = {UP: DOWN, DOWN: UP, LEFT: RIGHT, RIGHT: LEFT, UL: DR, UR: DL, DL: UR, DR: UL}


def poly(coefs, x):
    acc = jnp.full_like(x, coefs[-1])
    for c in coefs[-2::-1]:
        acc = acc * x + c
    return acc


def split(x):
    high = x.astype(jnp.bfloat16)
    low = (x - high.astype(jnp.float32)).astype(jnp.bfloat16)
    return high, low


def dot(a, b, dims):
    return lax.dot_general(a, b, (dims, ((), ())), preferred_element_type=jnp.float32)


def kernel(
    nb, nc, pd,
    panels_hbm, node_hbm, hoops_hbm, density_hbm, motion_hbm, force_hbm, stiff_hbm,
    density_out, pressure_out, motion_out,
    mot, frc, rows_in, cols_in, cols_own, stiff_in, kext, coef, onehot, rowhot,
    dens, press, wide, ga, gb, ga_src, pa, pb, pa_src, mats,
    sh_send, sh_recv, st_send, st_recv, a_send, a_recv, b_send, b_recv, pan_send, pan_recv,
    panels, node, hoops, density_in, motion_in, force_in, stiff, in_sems,
):
    f32 = jnp.float32
    b = lax.axis_index("blk")
    c = lax.axis_index("circ")
    axial, circum = stiff.shape
    last_tile = circum - 128
    cleft, cright = lax.rem(c + nc - 1, nc), lax.rem(c + 1, nc)
    where_to = {
        UP: (b - 1, c), DOWN: (b + 1, c), LEFT: (b, cleft), RIGHT: (b, cright),
        UL: (b - 1, cleft), UR: (b - 1, cright), DL: (b + 1, cleft), DR: (b + 1, cright),
    }
    has_up, has_down = b > 0, b < nb - 1

    def for_dirs(fn):
        fn(LEFT)
        fn(RIGHT)

        @pl.when(has_up)
        def _():
            for d in (UP, UL, UR):
                fn(d)

        @pl.when(has_down)
        def _():
            for d in (DOWN, DL, DR):
                fn(d)

    def for_peers(fn):
        if nb <= 8:
            for j in range(1, nb):
                fn(lax.rem(b + j, nb))
        else:
            def body(j, _):
                fn(lax.rem(b + j, nb))
                return 0

            lax.fori_loop(1, nb, body, 0)

    loads = [
        pltpu.make_async_copy(src, dst, in_sems.at[n])
        for n, (src, dst) in enumerate((
            (panels_hbm, panels), (density_hbm, density_in), (motion_hbm, motion_in),
            (stiff_hbm, stiff), (force_hbm, force_in), (node_hbm, node), (hoops_hbm, hoops),
        ))
    ]
    for load in loads:
        load.start()

    @pl.when(jnp.logical_not(has_up))
    def _():
        rows_in[:, 0] = jnp.zeros_like(rows_in[:, 0])
        cols_in[:, UL - 2] = jnp.zeros_like(cols_in[:, UL - 2])
        cols_in[:, UR - 2] = jnp.zeros_like(cols_in[:, UR - 2])
        stiff_in[UP] = jnp.zeros_like(stiff_in[UP])

    @pl.when(jnp.logical_not(has_down))
    def _():
        rows_in[:, 1] = jnp.zeros_like(rows_in[:, 1])
        cols_in[:, DL - 2] = jnp.zeros_like(cols_in[:, DL - 2])
        cols_in[:, DR - 2] = jnp.zeros_like(cols_in[:, DR - 2])
        stiff_in[DOWN] = jnp.zeros_like(stiff_in[DOWN])

    barrier = pltpu.get_barrier_semaphore()

    def greet(device):
        pl.semaphore_signal(barrier, inc=1, device_id=device, device_id_type=MESH)

    for j in range(1, nc):
        greet((b, lax.rem(c + j, nc)))
    for_peers(lambda peer: greet((peer, c)))

    @pl.when(has_up)
    def _():
        greet(where_to[UL])
        greet(where_to[UR])

    @pl.when(has_down)
    def _():
        greet(where_to[DL])
        greet(where_to[DR])

    lane = lax.broadcasted_iota(jnp.int32, (16, 128), 1)
    lane8 = lane[:8]

    def spread(x):
        x = jnp.where(lane[: x.shape[0]] < pd, x, 0.0)
        step = pd
        while step < 128:
            x = x + pltpu.roll(x, step, 1)
            step *= 2
        return x

    wide[...] = jnp.zeros_like(wide)
    loads[0].wait()
    loads[1].wait()
    wide[0:4, 0:pd] = panels[...]
    wide[8:24, 0:pd] = density_in[...]
    own = spread(wide[0:8, :])
    dens[...] = spread(wide[8:24, :])
    pa_src[...] = own
    ga_src[0] = dens[...].astype(jnp.bfloat16)

    pl.semaphore_wait(
        barrier,
        (nc - 1) + (nb - 1) + 2 * has_up.astype(jnp.int32) + 2 * has_down.astype(jnp.int32),
    )

    def copy(src, dst, send, recv, device):
        return pltpu.make_async_remote_copy(
            src_ref=src, dst_ref=dst, send_sem=send, recv_sem=recv,
            device_id=device, device_id_type=MESH,
        )

    me = (b, c)

    def a_start(rnd):
        for j in range(1, nc):
            copy(ga_src.at[rnd], ga.at[rnd, j - 1], a_send.at[rnd, j - 1], a_recv.at[rnd, j - 1],
                 (b, lax.rem(c + j, nc))).start()

    def a_wait(rnd):
        for j in range(1, nc):
            copy(ga_src.at[rnd], ga.at[rnd, j - 1], a_send.at[rnd, j - 1], a_recv.at[rnd, j - 1],
                 me).wait_recv()

    def merge(own_block, parts):
        group = lane[: own_block.shape[0]] // pd
        out = own_block
        for j in range(1, nc):
            out = jnp.where(group == lax.rem(c + nc - j, nc), parts[j - 1], out)
        return out

    def b_start(rnd):
        parts = [ga[rnd, j].astype(f32) for j in range(nc - 1)]
        gb[rnd, b] = merge(ga_src[rnd].astype(f32), parts).astype(jnp.bfloat16)
        for_peers(lambda peer: copy(gb.at[rnd, b], gb.at[rnd, b], b_send.at[rnd], b_recv.at[rnd],
                                    (peer, c)).start())

    def b_all(rnd):
        part = gb.at[rnd, pl.ds(0, nb - 1)]
        return copy(part, part, b_send.at[rnd], b_recv.at[rnd], me)

    for j in range(1, nc):
        copy(pa_src, pa.at[j - 1], pan_send.at[j - 1], pan_recv.at[j - 1],
             (b, lax.rem(c + j, nc))).start()
    a_start(0)
    loads[3].wait()
    stiff_dirs = (UP, DOWN, LEFT, RIGHT)

    def stiff_copy(d):
        return copy(stiff, stiff_in.at[OPPOSITE[d]], st_send.at[d], st_recv.at[OPPOSITE[d]],
                    where_to[d])

    for_dirs(lambda d: stiff_copy(d).start() if d in stiff_dirs else None)

    def shell_copy(s, d):
        o = OPPOSITE[d]
        if d in (UP, DOWN):
            src = mot.at[s, pl.ds(0 if d == UP else axial - 2, 2)]
            dst = rows_in.at[s, 0 if o == UP else 1]
        else:
            src, dst = cols_own.at[s], cols_in.at[s, o - 2]
        return copy(src, dst, sh_send.at[s, d], sh_recv.at[s, o], where_to[d])

    def shell_recv(s, d):
        if d in (UP, DOWN):
            dst = rows_in.at[s, 0 if d == UP else 1]
        else:
            dst = cols_in.at[s, d - 2]
        return copy(dst, dst, sh_send.at[s, d], sh_recv.at[s, d], me)

    place = (lane + 2) & 127
    row_of = ((128 - (place - (place & 3))) & 127) // 4

    def shell_start(s, rows):
        packed = None
        for r in range(axial):
            edge = jnp.where(lane < 64, rows[r][:, :128], rows[r][:, last_tile:])
            edge = pltpu.roll(edge, (128 - 4 * r) % 128, 1) if r else edge
            packed = edge if r == 0 else jnp.where(row_of == r, edge, packed)
        cols_own[s] = packed
        for_dirs(lambda d: shell_copy(s, d).start())

    loads[2].wait()
    first = []
    for r in range(axial):
        row = motion_in[:, r, :]
        mot[0, r] = row
        first.append(row)
    shell_start(0, first)
    for load in loads[4:]:
        load.wait()
    for r in range(axial):
        frc[r] = force_in[:, r, :]

    sub = lax.broadcasted_iota(jnp.int32, (axial, circum), 0) + b * axial
    hoop = jnp.zeros((axial, circum), f32)
    for h in range(hoops.shape[0]):
        hoop = jnp.where(sub == hoops[h], 1.0, hoop)
    k = stiff[...]
    shift = hoop_spring * hoop - inertia_term
    diag_re = 20.0 * k + shift
    diag_im = (20.0 * loss_factor) * k
    scale = relaxation / (diag_re * diag_re + diag_im * diag_im)
    inv_re, inv_im = diag_re * scale, diag_im * scale
    for r in range(axial):
        for n, x in enumerate((shift, inv_re, inv_im)):
            coef[n, r] = jnp.broadcast_to(x[r : r + 1], (8, circum))

    nodes = jnp.zeros((8, 128), jnp.int32)
    for p in range(pd):
        nodes = jnp.where((lane8 & (pd - 1)) == p, node[p], nodes)
    node_row = nodes // circum
    node_col = nodes - node_row * circum
    rowhot[...] = (node_row == lax.broadcasted_iota(jnp.int32, (8, 128), 0)).astype(f32)
    col_iota = lax.broadcasted_iota(jnp.int32, (circum, 128), 0)
    onehot[...] = (
        (jnp.broadcast_to(node_col[0:1], (circum, 128)) == col_iota).astype(f32).astype(jnp.bfloat16)
    )

    for j in range(1, nc):
        copy(pa_src, pa.at[j - 1], pan_send.at[j - 1], pan_recv.at[j - 1], me).wait_recv()
    a_wait(0)
    pb[b] = merge(pa_src[...], [pa[j] for j in range(nc - 1)])
    for_peers(lambda peer: copy(pb.at[b], pb.at[b], pan_send.at[nc - 1], pan_recv.at[nc - 1],
                                (peer, c)).start())
    b_start(0)
    pb_part = pb.at[pl.ds(0, nb - 1)]
    pb_all = copy(pb_part, pb_part, pan_send.at[nc - 1], pan_recv.at[nc - 1], me)

    for_dirs(
        lambda d: copy(stiff_in.at[d], stiff_in.at[d], st_send.at[d], st_recv.at[d], me).wait_recv()
        if d in stiff_dirs else None
    )
    right_tile = stiff_in[RIGHT][:, :128]
    left_tile = stiff_in[LEFT][:, last_tile:]
    side = jnp.where(lane8 < 64, right_tile, left_tile)
    k_up, k_down = stiff_in[UP], stiff_in[DOWN]
    for r in range(axial + 2):
        if r == 0:
            line = k_up[axial - 1 : axial]
        elif r == axial + 1:
            line = k_down[0:1]
        else:
            line = k[r - 1 : r]
            kext[r, :, circum:] = jnp.broadcast_to(side[r - 1 : r], (16, 128))
        kext[r, :, :circum] = jnp.broadcast_to(line, (16, circum))

    radial = jnp.sqrt(own[0:1] * own[0:1] + own[1:2] * own[1:2])
    eye = lax.broadcasted_iota(jnp.int32, (pd, 128), 0) == lax.broadcasted_iota(
        jnp.int32, (pd, 128), 1
    )

    def column(line):
        return jnp.sum(jnp.where(eye, jnp.broadcast_to(line, (pd, 128)), 0.0), axis=1, keepdims=True)

    tx, ty, tz = column(own[0:1]), column(own[1:2]), column(own[2:3])
    nx, ny = column(own[0:1] / radial), column(own[1:2] / radial)
    weight_row = own[3:4] * (pd * nb * nc / (8.0 * math.pi))

    pb_all.wait_recv()

    per = mats.shape[2] // 128
    for q in range(nb // per):
        for i in range(per):
            src = pb[q * per + i]
            dx, dy, dz = tx - src[0:1], ty - src[1:2], tz - src[2:3]
            area = src[3:4]
            dist_sq = dx * dx + dy * dy + dz * dz + area * (1.0 / math.pi)
            inverse = lax.rsqrt(dist_sq)
            phase = (wave_number * dist_sq) * inverse
            turns = phase * (1.0 / (2.0 * math.pi))
            turns = turns - jnp.round(turns)
            sq = turns * turns
            cosine = poly(COS, sq)
            sine = poly(SIN, sq) * turns
            weight = area * (1.0 / (4.0 * math.pi)) * inverse
            single = single_scale * weight
            double = double_scale * weight * (nx * dx + ny * dy) * inverse * inverse
            at = pl.ds(i * 128, 128)
            bf = jnp.bfloat16
            mats[q, 0:pd, at] = (single * cosine).astype(bf)
            mats[q, pd : 2 * pd, at] = (double * (-cosine - phase * sine)).astype(bf)
            mats[q, 2 * pd : 3 * pd, at] = (single * sine).astype(bf)
            mats[q, 3 * pd : 4 * pd, at] = (double * (phase * cosine - sine)).astype(bf)

    left_lanes = (lane & 3) >= 2

    def sweep(s):
        for_dirs(lambda d: shell_recv(s, d).wait_recv())
        tile = lambda d: cols_in[s, d - 2]
        side_own = jnp.where(left_lanes, tile(LEFT), tile(RIGHT))
        side_up = jnp.where(left_lanes, tile(UL), tile(UR))
        side_down = jnp.where(left_lanes, tile(DL), tile(DR))
        v = {}
        for r in range(axial):
            edge = pltpu.roll(side_own, 4 * r, 1) if r else side_own
            v[r] = jnp.concatenate([mot[s, r], edge], axis=1)
        v[-1] = jnp.concatenate([rows_in[s, 0, 1], pltpu.roll(side_up, 4 * (axial - 1), 1)], axis=1)
        v[axial] = jnp.concatenate([rows_in[s, 1, 0], side_down], axis=1)
        width = circum + 128

        def across(x):
            return pltpu.roll(x, 1, 1) + pltpu.roll(x, width - 1, 1) - 4.0 * x

        moment = {}
        for r in range(-1, axial + 1):
            if r == -1:
                lap = across(v[r])[:, :circum] + rows_in[s, 0, 0] + v[0][:, :circum]
            elif r == axial:
                lap = across(v[r])[:, :circum] + rows_in[s, 1, 1] + v[axial - 1][:, :circum]
            else:
                lap = across(v[r]) + v[r - 1] + v[r + 1]
            moment[r] = kext[r + 1, :, : lap.shape[1]] * lap
        out = []
        for r in range(axial):
            bend = (
                across(moment[r])[:, :circum]
                + moment[r - 1][:, :circum]
                + moment[r + 1][:, :circum]
            )
            here, load = mot[s, r], frc[axial + r]
            bend_re, bend_im = bend[:8], bend[8:]
            v_re, v_im = here[:8], here[8:]
            sh, a, m = coef[0, r], coef[1, r], coef[2, r]
            res_re = load[:8] - (bend_re - loss_factor * bend_im + sh * v_re)
            res_im = load[8:] - (bend_im + loss_factor * bend_re + sh * v_im)
            new = jnp.concatenate(
                [v_re + res_re * a + res_im * m, v_im + res_im * a - res_re * m], axis=0
            )
            mot[s + 1, r] = new
            out.append(new)
        return out

    def round_body(rnd, _):
        b_all(rnd).wait_recv()
        total = None
        for q in range(nb // per):
            block = jnp.concatenate([gb[rnd, q * per + i] for i in range(per)], axis=1)
            term = dot(block, mats[q], ((1,), (1,)))
            total = term if total is None else total + term
        re, im = total[:8], total[8:]
        both = jnp.concatenate(
            [re - pltpu.roll(im, 2 * pd, 1), im + pltpu.roll(re, 2 * pd, 1)], axis=0
        )
        pressure = spread(both)
        press[...] = pressure
        double = spread(pltpu.roll(both, 128 - pd, 1))
        s = SWEEPS * rnd
        neumann = jnp.zeros((16, 128), f32)
        picked = None
        for part in split(mot[s].reshape(axial * 16, circum)):
            term = dot(part, onehot[...], ((1,), (0,)))
            picked = term if picked is None else picked + term
        picked = picked.reshape(axial, 16, 128)
        for r in range(axial):
            neumann = neumann + picked[r] * rowhot[r : r + 1]
        density = 0.5 * dens[...] + neumann - double
        dens[...] = density

        @pl.when(rnd < ITERS - 1)
        def _():
            ga_src[rnd + 1] = density.astype(jnp.bfloat16)
            a_start(rnd + 1)

        weighted = jnp.where(lane < pd, pressure * weight_row, 0.0)
        spots = jnp.concatenate([weighted * rowhot[r : r + 1] for r in range(axial)], axis=0)
        fluid = None
        for part in split(spots):
            term = dot(part, onehot[...], ((1,), (1,)))
            fluid = term if fluid is None else fluid + term
        fluid = fluid.reshape(axial, 16, circum)
        for r in range(axial):
            frc[axial + r] = frc[r] - fluid[r]

        for i in range(SWEEPS):
            rows = sweep(s + i)
            if i < SWEEPS - 1:
                shell_start(s + i + 1, rows)

                @pl.when(rnd < ITERS - 1)
                def _():
                    a_wait(rnd + 1)
                    b_start(rnd + 1)
            else:
                @pl.when(rnd < ITERS - 1)
                def _():
                    shell_start(s + i + 1, rows)
        return 0

    lax.fori_loop(0, ITERS, round_body, 0)

    density_out[...] = dens[...][:, :pd]
    pressure_out[...] = press[...][:, :pd]
    for r in range(axial):
        motion_out[:, r, :] = mot[STEPS, r]

    for j in range(1, nc):
        copy(pa_src, pa.at[j - 1], pan_send.at[j - 1], pan_recv.at[j - 1], me).wait_send()
    pb_all.wait_send()
    for_dirs(lambda d: stiff_copy(d).wait_send() if d in stiff_dirs else None)

    def finish_round(rnd, _):
        for j in range(1, nc):
            copy(ga_src.at[rnd], ga.at[rnd, j - 1], a_send.at[rnd, j - 1], a_recv.at[rnd, j - 1],
                 me).wait_send()
        b_all(rnd).wait_send()
        for i in range(SWEEPS):
            for_dirs(lambda d: shell_copy(SWEEPS * rnd + i, d).wait_send())
        return 0

    lax.fori_loop(0, ITERS, finish_round, 0)


def per_device(nb, nc, panels, node, hoops, density, motion, force, stiffness):
    pd = panels.shape[1]
    channels, axial, circum = motion.shape
    per = math.gcd(nb, 8)
    f32, bf16 = jnp.float32, jnp.bfloat16
    vmem = pl.BlockSpec(memory_space=pltpu.VMEM)
    hbm = pl.BlockSpec(memory_space=pltpu.HBM)
    dma = pltpu.SemaphoreType.DMA
    scratch = [
        pltpu.VMEM((STEPS + 1, axial, channels, circum), f32),
        pltpu.VMEM((2 * axial, channels, circum), f32),
        pltpu.VMEM((STEPS, 2, 2, channels, circum), f32),
        pltpu.VMEM((STEPS, 6, channels, 128), f32),
        pltpu.VMEM((STEPS, channels, 128), f32),
        pltpu.VMEM((4, axial, circum), f32),
        pltpu.VMEM((axial + 2, channels, circum + 128), f32),
        pltpu.VMEM((3, axial, 8, circum), f32),
        pltpu.VMEM((circum, 128), bf16),
        pltpu.VMEM((8, 128), f32),
        pltpu.VMEM((channels, 128), f32),
        pltpu.VMEM((channels, 128), f32),
        pltpu.VMEM((24, 128), f32),
        pltpu.VMEM((ITERS, nc - 1, channels, 128), bf16),
        pltpu.VMEM((ITERS, nb, channels, 128), bf16),
        pltpu.VMEM((ITERS, channels, 128), bf16),
        pltpu.VMEM((nc - 1, 8, 128), f32),
        pltpu.VMEM((nb, 8, 128), f32),
        pltpu.VMEM((8, 128), f32),
        pltpu.VMEM((nb // per, 4 * pd, per * 128), bf16),
        dma((STEPS, 8)), dma((STEPS, 8)), dma((4,)), dma((4,)),
        dma((ITERS, nc - 1)), dma((ITERS, nc - 1)), dma((ITERS,)), dma((ITERS,)),
        dma((nc,)), dma((nc,)),
        pltpu.VMEM(panels.shape, f32), pltpu.SMEM(node.shape, jnp.int32),
        pltpu.SMEM(hoops.shape, jnp.int32), pltpu.VMEM(density.shape, f32),
        pltpu.VMEM(motion.shape, f32), pltpu.VMEM(force.shape, f32),
        pltpu.VMEM(stiffness.shape, f32), dma((7,)),
    ]
    return pl.pallas_call(
        functools.partial(kernel, nb, nc, pd),
        out_shape=(
            jax.ShapeDtypeStruct(density.shape, f32),
            jax.ShapeDtypeStruct(density.shape, f32),
            jax.ShapeDtypeStruct(motion.shape, f32),
        ),
        in_specs=[hbm] * 7,
        out_specs=(vmem, vmem, vmem),
        scratch_shapes=scratch,
        compiler_params=pltpu.CompilerParams(
            collective_id=0, has_side_effects=True, vmem_limit_bytes=64 * 1024 * 1024
        ),
    )(panels, node, hoops, density, motion, force, stiffness)


def solution(mesh):
    nb, nc = mesh.shape["blk"], mesh.shape["circ"]
    in_specs = (
        P(None, ("blk", "circ")),
        P(("blk", "circ")),
        P(),
        P(None, ("blk", "circ")),
        P(None, "blk", "circ"),
        P(None, "blk", "circ"),
        P("blk", "circ"),
    )
    out_specs = (P(None, ("blk", "circ")), P(None, ("blk", "circ")), P(None, "blk", "circ"))
    return jax.shard_map(
        functools.partial(per_device, nb, nc),
        mesh=mesh, in_specs=in_specs, out_specs=out_specs, check_vma=False,
    )
```

```python
import functools
import math

import jax
import jax.numpy as jnp
from jax import lax
from jax.experimental import pallas as pl
from jax.experimental.pallas import tpu as pltpu
from jax.sharding import PartitionSpec as P

MESH = pl.DeviceIdType.MESH
ITERS = 4
SWEEPS = 2
STEPS = ITERS * SWEEPS

wave_number = 4.0
single_scale = 30.0
double_scale = 6.0
hoop_spring = 40.0
inertia_term = 4.0
loss_factor = 0.2
relaxation = 0.3

COS = (
    0.9999999890590228, -19.739204499454, 64.93911745989914, -85.45013953093448,
    60.16763095128989, -25.96759924954187, 6.528658162606979,
)
SIN = (
    6.283185302511502, -41.34170040531754, 81.6051313857969, -76.70301535383193,
    42.02592698564183, -14.899846667160109, 3.2381375090822355,
)

UP, DOWN, LEFT, RIGHT, UL, UR, DL, DR = range(8)
OPPOSITE = {UP: DOWN, DOWN: UP, LEFT: RIGHT, RIGHT: LEFT, UL: DR, UR: DL, DL: UR, DR: UL}


def poly(coefs, x):
    acc = jnp.full_like(x, coefs[-1])
    for c in coefs[-2::-1]:
        acc = acc * x + c
    return acc


def split(x):
    high = x.astype(jnp.bfloat16)
    low = (x - high.astype(jnp.float32)).astype(jnp.bfloat16)
    return high, low


def dot(a, b, dims):
    return lax.dot_general(a, b, (dims, ((), ())), preferred_element_type=jnp.float32)


def kernel(
    nb, nc, pd,
    panels_hbm, node_hbm, hoops_hbm, density_hbm, motion_hbm, force_hbm, stiff_hbm,
    density_out, pressure_out, motion_out,
    mot, frc, rows_own, rows_in, cols_in, cols_own, stiff_in, kext, coef, onehot, rowhot,
    dens, press, wide, ga, gb, ga_src, pa, pb, pa_src, mats,
    sh_send, sh_recv, st_send, st_recv, a_send, a_recv, b_send, b_recv, pan_send, pan_recv,
    panels, node, hoops, density_in, motion_in, force_in, stiff, in_sems,
):
    f32 = jnp.float32
    b = lax.axis_index("blk")
    c = lax.axis_index("circ")
    axial, circum = stiff.shape
    last_tile = circum - 128
    cleft, cright = lax.rem(c + nc - 1, nc), lax.rem(c + 1, nc)
    where_to = {
        UP: (b - 1, c), DOWN: (b + 1, c), LEFT: (b, cleft), RIGHT: (b, cright),
        UL: (b - 1, cleft), UR: (b - 1, cright), DL: (b + 1, cleft), DR: (b + 1, cright),
    }
    has_up, has_down = b > 0, b < nb - 1

    def for_dirs(fn):
        @pl.when(has_up)
        def _():
            for d in (UP, UL, UR):
                fn(d)

        @pl.when(has_down)
        def _():
            for d in (DOWN, DL, DR):
                fn(d)

        fn(LEFT)
        fn(RIGHT)

    def for_peers(fn):
        if nb <= 8:
            for j in range(1, nb):
                fn(lax.rem(b + j, nb))
        else:
            def body(j, _):
                fn(lax.rem(b + j, nb))
                return 0

            lax.fori_loop(1, nb, body, 0)

    loads = [
        pltpu.make_async_copy(src, dst, in_sems.at[n])
        for n, (src, dst) in enumerate((
            (panels_hbm, panels), (density_hbm, density_in), (motion_hbm, motion_in),
            (stiff_hbm, stiff), (force_hbm, force_in), (node_hbm, node), (hoops_hbm, hoops),
        ))
    ]
    for load in loads:
        load.start()

    @pl.when(jnp.logical_not(has_up))
    def _():
        rows_in[:, 0] = jnp.zeros_like(rows_in[:, 0])
        cols_in[:, UL - 2] = jnp.zeros_like(cols_in[:, UL - 2])
        cols_in[:, UR - 2] = jnp.zeros_like(cols_in[:, UR - 2])
        stiff_in[UP] = jnp.zeros_like(stiff_in[UP])

    @pl.when(jnp.logical_not(has_down))
    def _():
        rows_in[:, 1] = jnp.zeros_like(rows_in[:, 1])
        cols_in[:, DL - 2] = jnp.zeros_like(cols_in[:, DL - 2])
        cols_in[:, DR - 2] = jnp.zeros_like(cols_in[:, DR - 2])
        stiff_in[DOWN] = jnp.zeros_like(stiff_in[DOWN])

    barrier = pltpu.get_barrier_semaphore()

    def greet(device):
        pl.semaphore_signal(barrier, inc=1, device_id=device, device_id_type=MESH)

    for j in range(1, nc):
        greet((b, lax.rem(c + j, nc)))
    for_peers(lambda peer: greet((peer, c)))

    @pl.when(has_up)
    def _():
        greet(where_to[UL])
        greet(where_to[UR])

    @pl.when(has_down)
    def _():
        greet(where_to[DL])
        greet(where_to[DR])

    lane = lax.broadcasted_iota(jnp.int32, (16, 128), 1)
    lane8 = lane[:8]

    def spread(x):
        x = jnp.where(lane[: x.shape[0]] < pd, x, 0.0)
        step = pd
        while step < 128:
            x = x + pltpu.roll(x, step, 1)
            step *= 2
        return x

    wide[...] = jnp.zeros_like(wide)
    loads[0].wait()
    loads[1].wait()
    wide[0:4, 0:pd] = panels[...]
    wide[8:24, 0:pd] = density_in[...]
    own = spread(wide[0:8, :])
    dens[...] = spread(wide[8:24, :])
    pa_src[...] = own
    ga_src[0] = dens[...].astype(jnp.bfloat16)

    pl.semaphore_wait(
        barrier,
        (nc - 1) + (nb - 1) + 2 * has_up.astype(jnp.int32) + 2 * has_down.astype(jnp.int32),
    )

    def copy(src, dst, send, recv, device):
        return pltpu.make_async_remote_copy(
            src_ref=src, dst_ref=dst, send_sem=send, recv_sem=recv,
            device_id=device, device_id_type=MESH,
        )

    me = (b, c)

    def a_start(rnd):
        for j in range(1, nc):
            copy(ga_src.at[rnd], ga.at[rnd, j - 1], a_send.at[rnd, j - 1], a_recv.at[rnd, j - 1],
                 (b, lax.rem(c + j, nc))).start()

    def a_wait(rnd):
        for j in range(1, nc):
            copy(ga_src.at[rnd], ga.at[rnd, j - 1], a_send.at[rnd, j - 1], a_recv.at[rnd, j - 1],
                 me).wait_recv()

    def merge(own_block, parts):
        group = lane[: own_block.shape[0]] // pd
        out = own_block
        for j in range(1, nc):
            out = jnp.where(group == lax.rem(c + nc - j, nc), parts[j - 1], out)
        return out

    def b_start(rnd):
        parts = [ga[rnd, j].astype(f32) for j in range(nc - 1)]
        gb[rnd, b] = merge(ga_src[rnd].astype(f32), parts).astype(jnp.bfloat16)
        for_peers(lambda peer: copy(gb.at[rnd, b], gb.at[rnd, b], b_send.at[rnd], b_recv.at[rnd],
                                    (peer, c)).start())

    def b_all(rnd):
        part = gb.at[rnd, pl.ds(0, nb - 1)]
        return copy(part, part, b_send.at[rnd], b_recv.at[rnd], me)

    for j in range(1, nc):
        copy(pa_src, pa.at[j - 1], pan_send.at[j - 1], pan_recv.at[j - 1],
             (b, lax.rem(c + j, nc))).start()
    a_start(0)
    loads[3].wait()
    stiff_dirs = (UP, DOWN, LEFT, RIGHT)

    def stiff_copy(d):
        return copy(stiff, stiff_in.at[OPPOSITE[d]], st_send.at[d], st_recv.at[OPPOSITE[d]],
                    where_to[d])

    for_dirs(lambda d: stiff_copy(d).start() if d in stiff_dirs else None)

    def shell_copy(s, d):
        o = OPPOSITE[d]
        if d in (UP, DOWN):
            src = rows_own.at[s, 0 if d == UP else 1]
            dst = rows_in.at[s, 0 if o == UP else 1]
        else:
            src, dst = cols_own.at[s], cols_in.at[s, o - 2]
        return copy(src, dst, sh_send.at[s, d], sh_recv.at[s, o], where_to[d])

    def shell_recv(s, d):
        if d in (UP, DOWN):
            dst = rows_in.at[s, 0 if d == UP else 1]
        else:
            dst = cols_in.at[s, d - 2]
        return copy(dst, dst, sh_send.at[s, d], sh_recv.at[s, d], me)

    place = (lane + 2) & 127
    row_of = ((128 - (place - (place & 3))) & 127) // 4

    def shell_start(s, rows):
        packed = None
        for r in range(axial):
            edge = jnp.where(lane < 64, rows[r][:, :128], rows[r][:, last_tile:])
            edge = pltpu.roll(edge, (128 - 4 * r) % 128, 1) if r else edge
            packed = edge if r == 0 else jnp.where(row_of == r, edge, packed)
        bf = jnp.bfloat16
        cols_own[s] = packed.astype(bf)
        for n, at in enumerate((0, axial - 2)):
            for i in range(2):
                rows_own[s, n, i] = rows[at + i].astype(bf)
        for_dirs(lambda d: shell_copy(s, d).start())

    loads[2].wait()
    first = []
    for r in range(axial):
        row = motion_in[:, r, :]
        mot[0, r] = row
        first.append(row)
    shell_start(0, first)
    for load in loads[4:]:
        load.wait()
    for r in range(axial):
        frc[r] = force_in[:, r, :]

    sub = lax.broadcasted_iota(jnp.int32, (axial, circum), 0) + b * axial
    hoop = jnp.zeros((axial, circum), f32)
    for h in range(hoops.shape[0]):
        hoop = jnp.where(sub == hoops[h], 1.0, hoop)
    k = stiff[...]
    shift = hoop_spring * hoop - inertia_term
    diag_re = 20.0 * k + shift
    diag_im = (20.0 * loss_factor) * k
    scale = relaxation / (diag_re * diag_re + diag_im * diag_im)
    inv_re, inv_im = diag_re * scale, diag_im * scale
    for r in range(axial):
        for n, x in enumerate((shift, inv_re, inv_im)):
            coef[n, r] = jnp.broadcast_to(x[r : r + 1], (8, circum))

    nodes = jnp.zeros((8, 128), jnp.int32)
    for p in range(pd):
        nodes = jnp.where((lane8 & (pd - 1)) == p, node[p], nodes)
    node_row = nodes // circum
    node_col = nodes - node_row * circum
    rowhot[...] = (node_row == lax.broadcasted_iota(jnp.int32, (8, 128), 0)).astype(f32)
    col_iota = lax.broadcasted_iota(jnp.int32, (circum, 128), 0)
    onehot[...] = (
        (jnp.broadcast_to(node_col[0:1], (circum, 128)) == col_iota).astype(f32).astype(jnp.bfloat16)
    )

    for j in range(1, nc):
        copy(pa_src, pa.at[j - 1], pan_send.at[j - 1], pan_recv.at[j - 1], me).wait_recv()
    a_wait(0)
    pb[b] = merge(pa_src[...], [pa[j] for j in range(nc - 1)])
    for_peers(lambda peer: copy(pb.at[b], pb.at[b], pan_send.at[nc - 1], pan_recv.at[nc - 1],
                                (peer, c)).start())
    b_start(0)
    pb_part = pb.at[pl.ds(0, nb - 1)]
    pb_all = copy(pb_part, pb_part, pan_send.at[nc - 1], pan_recv.at[nc - 1], me)

    for_dirs(
        lambda d: copy(stiff_in.at[d], stiff_in.at[d], st_send.at[d], st_recv.at[d], me).wait_recv()
        if d in stiff_dirs else None
    )
    right_tile = stiff_in[RIGHT][:, :128]
    left_tile = stiff_in[LEFT][:, last_tile:]
    side = jnp.where(lane8 < 64, right_tile, left_tile)
    k_up, k_down = stiff_in[UP], stiff_in[DOWN]
    for r in range(axial + 2):
        if r == 0:
            line = k_up[axial - 1 : axial]
        elif r == axial + 1:
            line = k_down[0:1]
        else:
            line = k[r - 1 : r]
            kext[r, :, circum:] = jnp.broadcast_to(side[r - 1 : r], (16, 128))
        kext[r, :, :circum] = jnp.broadcast_to(line, (16, circum))

    radial = jnp.sqrt(own[0:1] * own[0:1] + own[1:2] * own[1:2])
    eye = lax.broadcasted_iota(jnp.int32, (pd, 128), 0) == lax.broadcasted_iota(
        jnp.int32, (pd, 128), 1
    )

    def column(line):
        return jnp.sum(jnp.where(eye, jnp.broadcast_to(line, (pd, 128)), 0.0), axis=1, keepdims=True)

    tx, ty, tz = column(own[0:1]), column(own[1:2]), column(own[2:3])
    nx, ny = column(own[0:1] / radial), column(own[1:2] / radial)
    weight_row = own[3:4] * (pd * nb * nc / (8.0 * math.pi))

    pb_all.wait_recv()

    per = mats.shape[2] // 128
    for q in range(nb // per):
        for i in range(per):
            src = pb[q * per + i]
            dx, dy, dz = tx - src[0:1], ty - src[1:2], tz - src[2:3]
            area = src[3:4]
            dist_sq = dx * dx + dy * dy + dz * dz + area * (1.0 / math.pi)
            inverse = lax.rsqrt(dist_sq)
            phase = (wave_number * dist_sq) * inverse
            turns = phase * (1.0 / (2.0 * math.pi))
            turns = turns - jnp.round(turns)
            sq = turns * turns
            cosine = poly(COS, sq)
            sine = poly(SIN, sq) * turns
            weight = area * (1.0 / (4.0 * math.pi)) * inverse
            single = single_scale * weight
            double = double_scale * weight * (nx * dx + ny * dy) * inverse * inverse
            at = pl.ds(i * 128, 128)
            bf = jnp.bfloat16
            mats[q, 0:pd, at] = (single * cosine).astype(bf)
            mats[q, pd : 2 * pd, at] = (double * (-cosine - phase * sine)).astype(bf)
            mats[q, 2 * pd : 3 * pd, at] = (single * sine).astype(bf)
            mats[q, 3 * pd : 4 * pd, at] = (double * (phase * cosine - sine)).astype(bf)

    left_lanes = (lane & 3) >= 2

    def sweep(s):
        for_dirs(lambda d: shell_recv(s, d).wait_recv())
        tile = lambda d: cols_in[s, d - 2].astype(f32)
        side_own = jnp.where(left_lanes, tile(LEFT), tile(RIGHT))
        side_up = jnp.where(left_lanes, tile(UL), tile(UR))
        side_down = jnp.where(left_lanes, tile(DL), tile(DR))
        above = [rows_in[s, 0, i].astype(f32) for i in range(2)]
        below = [rows_in[s, 1, i].astype(f32) for i in range(2)]
        v = {}
        for r in range(axial):
            edge = pltpu.roll(side_own, 4 * r, 1) if r else side_own
            v[r] = jnp.concatenate([mot[s, r], edge], axis=1)
        v[-1] = jnp.concatenate([above[1], pltpu.roll(side_up, 4 * (axial - 1), 1)], axis=1)
        v[axial] = jnp.concatenate([below[0], side_down], axis=1)
        width = circum + 128

        def across(x):
            return pltpu.roll(x, 1, 1) + pltpu.roll(x, width - 1, 1) - 4.0 * x

        moment = {}
        for r in range(-1, axial + 1):
            if r == -1:
                lap = across(v[r])[:, :circum] + above[0] + v[0][:, :circum]
            elif r == axial:
                lap = across(v[r])[:, :circum] + below[1] + v[axial - 1][:, :circum]
            else:
                lap = across(v[r]) + v[r - 1] + v[r + 1]
            moment[r] = kext[r + 1, :, : lap.shape[1]] * lap
        out = []
        for r in range(axial):
            bend = (
                across(moment[r])[:, :circum]
                + moment[r - 1][:, :circum]
                + moment[r + 1][:, :circum]
            )
            here, load = mot[s, r], frc[axial + r]
            bend_re, bend_im = bend[:8], bend[8:]
            v_re, v_im = here[:8], here[8:]
            sh, a, m = coef[0, r], coef[1, r], coef[2, r]
            res_re = load[:8] - (bend_re - loss_factor * bend_im + sh * v_re)
            res_im = load[8:] - (bend_im + loss_factor * bend_re + sh * v_im)
            new = jnp.concatenate(
                [v_re + res_re * a + res_im * m, v_im + res_im * a - res_re * m], axis=0
            )
            mot[s + 1, r] = new
            out.append(new)
        return out

    def round_body(rnd, _):
        b_all(rnd).wait_recv()
        total = None
        for q in range(nb // per):
            block = jnp.concatenate([gb[rnd, q * per + i] for i in range(per)], axis=1)
            term = dot(block, mats[q], ((1,), (1,)))
            total = term if total is None else total + term
        re, im = total[:8], total[8:]
        both = jnp.concatenate(
            [re - pltpu.roll(im, 2 * pd, 1), im + pltpu.roll(re, 2 * pd, 1)], axis=0
        )
        pressure = spread(both)
        press[...] = pressure
        double = spread(pltpu.roll(both, 128 - pd, 1))
        s = SWEEPS * rnd
        neumann = jnp.zeros((16, 128), f32)
        picked = None
        for part in split(mot[s].reshape(axial * 16, circum)):
            term = dot(part, onehot[...], ((1,), (0,)))
            picked = term if picked is None else picked + term
        picked = picked.reshape(axial, 16, 128)
        for r in range(axial):
            neumann = neumann + picked[r] * rowhot[r : r + 1]
        density = 0.5 * dens[...] + neumann - double
        dens[...] = density

        @pl.when(rnd < ITERS - 1)
        def _():
            ga_src[rnd + 1] = density.astype(jnp.bfloat16)
            a_start(rnd + 1)

        weighted = jnp.where(lane < pd, pressure * weight_row, 0.0)
        spots = jnp.concatenate([weighted * rowhot[r : r + 1] for r in range(axial)], axis=0)
        fluid = None
        for part in split(spots):
            term = dot(part, onehot[...], ((1,), (1,)))
            fluid = term if fluid is None else fluid + term
        fluid = fluid.reshape(axial, 16, circum)
        for r in range(axial):
            frc[axial + r] = frc[r] - fluid[r]

        for i in range(SWEEPS):
            rows = sweep(s + i)
            if i < SWEEPS - 1:
                shell_start(s + i + 1, rows)

                @pl.when(rnd < ITERS - 1)
                def _():
                    a_wait(rnd + 1)
                    b_start(rnd + 1)
            else:
                @pl.when(rnd < ITERS - 1)
                def _():
                    shell_start(s + i + 1, rows)
        return 0

    lax.fori_loop(0, ITERS, round_body, 0)

    density_out[...] = dens[...][:, :pd]
    pressure_out[...] = press[...][:, :pd]
    for r in range(axial):
        motion_out[:, r, :] = mot[STEPS, r]

    for j in range(1, nc):
        copy(pa_src, pa.at[j - 1], pan_send.at[j - 1], pan_recv.at[j - 1], me).wait_send()
    pb_all.wait_send()
    for_dirs(lambda d: stiff_copy(d).wait_send() if d in stiff_dirs else None)

    def finish_round(rnd, _):
        for j in range(1, nc):
            copy(ga_src.at[rnd], ga.at[rnd, j - 1], a_send.at[rnd, j - 1], a_recv.at[rnd, j - 1],
                 me).wait_send()
        b_all(rnd).wait_send()
        for i in range(SWEEPS):
            for_dirs(lambda d: shell_copy(SWEEPS * rnd + i, d).wait_send())
        return 0

    lax.fori_loop(0, ITERS, finish_round, 0)


def per_device(nb, nc, panels, node, hoops, density, motion, force, stiffness):
    pd = panels.shape[1]
    channels, axial, circum = motion.shape
    per = math.gcd(nb, 8)
    f32, bf16 = jnp.float32, jnp.bfloat16
    vmem = pl.BlockSpec(memory_space=pltpu.VMEM)
    hbm = pl.BlockSpec(memory_space=pltpu.HBM)
    dma = pltpu.SemaphoreType.DMA
    scratch = [
        pltpu.VMEM((STEPS + 1, axial, channels, circum), f32),
        pltpu.VMEM((2 * axial, channels, circum), f32),
        pltpu.VMEM((STEPS, 2, 2, channels, circum), bf16),
        pltpu.VMEM((STEPS, 2, 2, channels, circum), bf16),
        pltpu.VMEM((STEPS, 6, channels, 128), bf16),
        pltpu.VMEM((STEPS, channels, 128), bf16),
        pltpu.VMEM((4, axial, circum), f32),
        pltpu.VMEM((axial + 2, channels, circum + 128), f32),
        pltpu.VMEM((3, axial, 8, circum), f32),
        pltpu.VMEM((circum, 128), bf16),
        pltpu.VMEM((8, 128), f32),
        pltpu.VMEM((channels, 128), f32),
        pltpu.VMEM((channels, 128), f32),
        pltpu.VMEM((24, 128), f32),
        pltpu.VMEM((ITERS, nc - 1, channels, 128), bf16),
        pltpu.VMEM((ITERS, nb, channels, 128), bf16),
        pltpu.VMEM((ITERS, channels, 128), bf16),
        pltpu.VMEM((nc - 1, 8, 128), f32),
        pltpu.VMEM((nb, 8, 128), f32),
        pltpu.VMEM((8, 128), f32),
        pltpu.VMEM((nb // per, 4 * pd, per * 128), bf16),
        dma((STEPS, 8)), dma((STEPS, 8)), dma((4,)), dma((4,)),
        dma((ITERS, nc - 1)), dma((ITERS, nc - 1)), dma((ITERS,)), dma((ITERS,)),
        dma((nc,)), dma((nc,)),
        pltpu.VMEM(panels.shape, f32), pltpu.SMEM(node.shape, jnp.int32),
        pltpu.SMEM(hoops.shape, jnp.int32), pltpu.VMEM(density.shape, f32),
        pltpu.VMEM(motion.shape, f32), pltpu.VMEM(force.shape, f32),
        pltpu.VMEM(stiffness.shape, f32), dma((7,)),
    ]
    return pl.pallas_call(
        functools.partial(kernel, nb, nc, pd),
        out_shape=(
            jax.ShapeDtypeStruct(density.shape, f32),
            jax.ShapeDtypeStruct(density.shape, f32),
            jax.ShapeDtypeStruct(motion.shape, f32),
        ),
        in_specs=[hbm] * 7,
        out_specs=(vmem, vmem, vmem),
        scratch_shapes=scratch,
        compiler_params=pltpu.CompilerParams(
            collective_id=0, has_side_effects=True, vmem_limit_bytes=64 * 1024 * 1024
        ),
    )(panels, node, hoops, density, motion, force, stiffness)


def solution(mesh):
    nb, nc = mesh.shape["blk"], mesh.shape["circ"]
    in_specs = (
        P(None, ("blk", "circ")),
        P(("blk", "circ")),
        P(),
        P(None, ("blk", "circ")),
        P(None, "blk", "circ"),
        P(None, "blk", "circ"),
        P("blk", "circ"),
    )
    out_specs = (P(None, ("blk", "circ")), P(None, ("blk", "circ")), P(None, "blk", "circ"))
    return jax.shard_map(
        functools.partial(per_device, nb, nc),
        mesh=mesh, in_specs=in_specs, out_specs=out_specs, check_vma=False,
    )
```

```python
import functools
import math

import jax
import jax.numpy as jnp
from jax import lax
from jax.experimental import pallas as pl
from jax.experimental.pallas import tpu as pltpu
from jax.sharding import PartitionSpec as P

MESH = pl.DeviceIdType.MESH
ITERS = 4
SWEEPS = 2
STEPS = ITERS * SWEEPS

wave_number = 4.0
single_scale = 30.0
double_scale = 6.0
hoop_spring = 40.0
inertia_term = 4.0
loss_factor = 0.2
relaxation = 0.3

COS = (
    0.9999999890590228, -19.739204499454, 64.93911745989914, -85.45013953093448,
    60.16763095128989, -25.96759924954187, 6.528658162606979,
)
SIN = (
    6.283185302511502, -41.34170040531754, 81.6051313857969, -76.70301535383193,
    42.02592698564183, -14.899846667160109, 3.2381375090822355,
)

UP, DOWN, LEFT, RIGHT, UL, UR, DL, DR = range(8)
OPPOSITE = {UP: DOWN, DOWN: UP, LEFT: RIGHT, RIGHT: LEFT, UL: DR, UR: DL, DL: UR, DR: UL}


def poly(coefs, x):
    acc = jnp.full_like(x, coefs[-1])
    for c in coefs[-2::-1]:
        acc = acc * x + c
    return acc


def split(x):
    high = x.astype(jnp.bfloat16)
    low = (x - high.astype(jnp.float32)).astype(jnp.bfloat16)
    return high, low


def dot(a, b, dims):
    return lax.dot_general(a, b, (dims, ((), ())), preferred_element_type=jnp.float32)


def kernel(
    nb, nc, pd,
    panels_hbm, node_hbm, hoops_hbm, density_hbm, motion_hbm, force_hbm, stiff_hbm,
    density_out, pressure_out, motion_out,
    mot, frc, rows_own, rows_in, cols_in, cols_own, stiff_in, kext, coef, onehot, rowhot,
    dens, press, wide, ga, gb, ga_src, pa, pb, pa_src, mats,
    sh_send, sh_recv, st_send, st_recv, a_send, a_recv, b_send, b_recv, pan_send, pan_recv,
    panels, node, hoops, density_in, motion_in, force_in, stiff, in_sems,
):
    f32 = jnp.float32
    b = lax.axis_index("blk")
    c = lax.axis_index("circ")
    axial, circum = stiff.shape
    last_tile = circum - 128
    cleft, cright = lax.rem(c + nc - 1, nc), lax.rem(c + 1, nc)
    where_to = {
        UP: (b - 1, c), DOWN: (b + 1, c), LEFT: (b, cleft), RIGHT: (b, cright),
        UL: (b - 1, cleft), UR: (b - 1, cright), DL: (b + 1, cleft), DR: (b + 1, cright),
    }
    has_up, has_down = b > 0, b < nb - 1

    def for_dirs(fn):
        @pl.when(has_up)
        def _():
            for d in (UP, UL, UR):
                fn(d)

        @pl.when(has_down)
        def _():
            for d in (DOWN, DL, DR):
                fn(d)

        fn(LEFT)
        fn(RIGHT)

    def for_peers(fn):
        if nb <= 8:
            for j in range(1, nb):
                fn(lax.rem(b + j, nb))
        else:
            def body(j, _):
                fn(lax.rem(b + j, nb))
                return 0

            lax.fori_loop(1, nb, body, 0)

    loads = [
        pltpu.make_async_copy(src, dst, in_sems.at[n])
        for n, (src, dst) in enumerate((
            (panels_hbm, panels), (density_hbm, density_in), (motion_hbm, motion_in),
            (stiff_hbm, stiff), (force_hbm, force_in), (node_hbm, node), (hoops_hbm, hoops),
        ))
    ]
    for load in loads:
        load.start()

    @pl.when(jnp.logical_not(has_up))
    def _():
        rows_in[:, 0] = jnp.zeros_like(rows_in[:, 0])
        cols_in[:, UL - 2] = jnp.zeros_like(cols_in[:, UL - 2])
        cols_in[:, UR - 2] = jnp.zeros_like(cols_in[:, UR - 2])
        stiff_in[UP] = jnp.zeros_like(stiff_in[UP])

    @pl.when(jnp.logical_not(has_down))
    def _():
        rows_in[:, 1] = jnp.zeros_like(rows_in[:, 1])
        cols_in[:, DL - 2] = jnp.zeros_like(cols_in[:, DL - 2])
        cols_in[:, DR - 2] = jnp.zeros_like(cols_in[:, DR - 2])
        stiff_in[DOWN] = jnp.zeros_like(stiff_in[DOWN])

    barrier = pltpu.get_barrier_semaphore()

    def greet(device):
        pl.semaphore_signal(barrier, inc=1, device_id=device, device_id_type=MESH)

    for j in range(1, nc):
        greet((b, lax.rem(c + j, nc)))
    for_peers(lambda peer: greet((peer, c)))

    @pl.when(has_up)
    def _():
        greet(where_to[UL])
        greet(where_to[UR])

    @pl.when(has_down)
    def _():
        greet(where_to[DL])
        greet(where_to[DR])

    lane = lax.broadcasted_iota(jnp.int32, (16, 128), 1)
    lane8 = lane[:8]

    def spread(x):
        x = jnp.where(lane[: x.shape[0]] < pd, x, 0.0)
        step = pd
        while step < 128:
            x = x + pltpu.roll(x, step, 1)
            step *= 2
        return x

    wide[...] = jnp.zeros_like(wide)
    loads[0].wait()
    loads[1].wait()
    wide[0:4, 0:pd] = panels[...]
    wide[8:24, 0:pd] = density_in[...]
    own = spread(wide[0:8, :])
    dens[...] = spread(wide[8:24, :])
    pa_src[...] = own
    ga_src[0] = dens[...].astype(jnp.bfloat16)

    pl.semaphore_wait(
        barrier,
        (nc - 1) + (nb - 1) + 2 * has_up.astype(jnp.int32) + 2 * has_down.astype(jnp.int32),
    )

    def copy(src, dst, send, recv, device):
        return pltpu.make_async_remote_copy(
            src_ref=src, dst_ref=dst, send_sem=send, recv_sem=recv,
            device_id=device, device_id_type=MESH,
        )

    me = (b, c)

    def a_start(rnd):
        for j in range(1, nc):
            copy(ga_src.at[rnd], ga.at[rnd, j - 1], a_send.at[rnd, j - 1], a_recv.at[rnd, j - 1],
                 (b, lax.rem(c + j, nc))).start()

    def a_wait(rnd):
        for j in range(1, nc):
            copy(ga_src.at[rnd], ga.at[rnd, j - 1], a_send.at[rnd, j - 1], a_recv.at[rnd, j - 1],
                 me).wait_recv()

    def merge(own_block, parts):
        group = lane[: own_block.shape[0]] // pd
        out = own_block
        for j in range(1, nc):
            out = jnp.where(group == lax.rem(c + nc - j, nc), parts[j - 1], out)
        return out

    def b_start(rnd):
        parts = [ga[rnd, j].astype(f32) for j in range(nc - 1)]
        gb[rnd, b] = merge(ga_src[rnd].astype(f32), parts).astype(jnp.bfloat16)
        for_peers(lambda peer: copy(gb.at[rnd, b], gb.at[rnd, b], b_send.at[rnd], b_recv.at[rnd],
                                    (peer, c)).start())

    def b_all(rnd):
        part = gb.at[rnd, pl.ds(0, nb - 1)]
        return copy(part, part, b_send.at[rnd], b_recv.at[rnd], me)

    for j in range(1, nc):
        copy(pa_src, pa.at[j - 1], pan_send.at[j - 1], pan_recv.at[j - 1],
             (b, lax.rem(c + j, nc))).start()
    a_start(0)
    loads[3].wait()
    stiff_dirs = (UP, DOWN, LEFT, RIGHT)

    def stiff_copy(d):
        return copy(stiff, stiff_in.at[OPPOSITE[d]], st_send.at[d], st_recv.at[OPPOSITE[d]],
                    where_to[d])

    for_dirs(lambda d: stiff_copy(d).start() if d in stiff_dirs else None)

    def shell_copy(s, d):
        o = OPPOSITE[d]
        if d in (UP, DOWN):
            src = rows_own.at[s, 0 if d == UP else 1]
            dst = rows_in.at[s, 0 if o == UP else 1]
        else:
            src, dst = cols_own.at[s], cols_in.at[s, o - 2]
        return copy(src, dst, sh_send.at[s, d], sh_recv.at[s, o], where_to[d])

    def shell_recv(s, d):
        if d in (UP, DOWN):
            dst = rows_in.at[s, 0 if d == UP else 1]
        else:
            dst = cols_in.at[s, d - 2]
        return copy(dst, dst, sh_send.at[s, d], sh_recv.at[s, d], me)

    place = (lane + 2) & 127
    row_of = ((128 - (place - (place & 3))) & 127) // 4

    def shell_start(s, rows):
        packed = None
        for r in range(axial):
            edge = jnp.where(lane < 64, rows[r][:, :128], rows[r][:, last_tile:])
            edge = pltpu.roll(edge, (128 - 4 * r) % 128, 1) if r else edge
            packed = edge if r == 0 else jnp.where(row_of == r, edge, packed)
        bf = jnp.bfloat16
        cols_own[s] = packed.astype(bf)
        for n, at in enumerate((0, axial - 2)):
            for i in range(2):
                rows_own[s, n, i] = rows[at + i].astype(bf)
        for_dirs(lambda d: shell_copy(s, d).start())

    loads[2].wait()
    first = []
    for r in range(axial):
        row = motion_in[:, r, :]
        mot[0, r] = row
        first.append(row)
    shell_start(0, first)
    for load in loads[4:]:
        load.wait()
    for r in range(axial):
        frc[r] = force_in[:, r, :]

    sub = lax.broadcasted_iota(jnp.int32, (axial, circum), 0) + b * axial
    hoop = jnp.zeros((axial, circum), f32)
    for h in range(hoops.shape[0]):
        hoop = jnp.where(sub == hoops[h], 1.0, hoop)
    k = stiff[...]
    shift = hoop_spring * hoop - inertia_term
    diag_re = 20.0 * k + shift
    diag_im = (20.0 * loss_factor) * k
    scale = relaxation / (diag_re * diag_re + diag_im * diag_im)
    inv_re, inv_im = diag_re * scale, diag_im * scale
    for r in range(axial):
        for n, x in enumerate((shift, inv_re, inv_im)):
            coef[n, r] = jnp.broadcast_to(x[r : r + 1], (8, circum))

    nodes = jnp.zeros((8, 128), jnp.int32)
    for p in range(pd):
        nodes = jnp.where((lane8 & (pd - 1)) == p, node[p], nodes)
    node_row = nodes // circum
    node_col = nodes - node_row * circum
    rowhot[...] = (node_row == lax.broadcasted_iota(jnp.int32, (8, 128), 0)).astype(f32)
    col_iota = lax.broadcasted_iota(jnp.int32, (circum, 128), 0)
    onehot[...] = (
        (jnp.broadcast_to(node_col[0:1], (circum, 128)) == col_iota).astype(f32).astype(jnp.bfloat16)
    )

    for j in range(1, nc):
        copy(pa_src, pa.at[j - 1], pan_send.at[j - 1], pan_recv.at[j - 1], me).wait_recv()
    a_wait(0)
    pb[b] = merge(pa_src[...], [pa[j] for j in range(nc - 1)])
    for_peers(lambda peer: copy(pb.at[b], pb.at[b], pan_send.at[nc - 1], pan_recv.at[nc - 1],
                                (peer, c)).start())
    b_start(0)
    pb_part = pb.at[pl.ds(0, nb - 1)]
    pb_all = copy(pb_part, pb_part, pan_send.at[nc - 1], pan_recv.at[nc - 1], me)

    for_dirs(
        lambda d: copy(stiff_in.at[d], stiff_in.at[d], st_send.at[d], st_recv.at[d], me).wait_recv()
        if d in stiff_dirs else None
    )
    right_tile = stiff_in[RIGHT][:, :128]
    left_tile = stiff_in[LEFT][:, last_tile:]
    side = jnp.where(lane8 < 64, right_tile, left_tile)
    k_up, k_down = stiff_in[UP], stiff_in[DOWN]
    for r in range(axial + 2):
        if r == 0:
            line = k_up[axial - 1 : axial]
        elif r == axial + 1:
            line = k_down[0:1]
        else:
            line = k[r - 1 : r]
            kext[r, :, circum:] = jnp.broadcast_to(side[r - 1 : r], (16, 128))
        kext[r, :, :circum] = jnp.broadcast_to(line, (16, circum))

    radial = jnp.sqrt(own[0:1] * own[0:1] + own[1:2] * own[1:2])
    eye = lax.broadcasted_iota(jnp.int32, (pd, 128), 0) == lax.broadcasted_iota(
        jnp.int32, (pd, 128), 1
    )

    def column(line):
        return jnp.sum(jnp.where(eye, jnp.broadcast_to(line, (pd, 128)), 0.0), axis=1, keepdims=True)

    tx, ty, tz = column(own[0:1]), column(own[1:2]), column(own[2:3])
    nx, ny = column(own[0:1] / radial), column(own[1:2] / radial)
    weight_row = own[3:4] * (pd * nb * nc / (8.0 * math.pi))

    pb_all.wait_recv()

    per = mats.shape[2] // 128
    for q in range(nb // per):
        for i in range(per):
            src = pb[q * per + i]
            dx, dy, dz = tx - src[0:1], ty - src[1:2], tz - src[2:3]
            area = src[3:4]
            dist_sq = dx * dx + dy * dy + dz * dz + area * (1.0 / math.pi)
            inverse = lax.rsqrt(dist_sq)
            phase = (wave_number * dist_sq) * inverse
            turns = phase * (1.0 / (2.0 * math.pi))
            turns = turns - jnp.round(turns)
            sq = turns * turns
            cosine = poly(COS, sq)
            sine = poly(SIN, sq) * turns
            weight = area * (1.0 / (4.0 * math.pi)) * inverse
            single = single_scale * weight
            double = double_scale * weight * (nx * dx + ny * dy) * inverse * inverse
            at = pl.ds(i * 128, 128)
            bf = jnp.bfloat16
            mats[q, 0:pd, at] = (single * cosine).astype(bf)
            mats[q, pd : 2 * pd, at] = (double * (-cosine - phase * sine)).astype(bf)
            mats[q, 2 * pd : 3 * pd, at] = (single * sine).astype(bf)
            mats[q, 3 * pd : 4 * pd, at] = (double * (phase * cosine - sine)).astype(bf)

    left_lanes = (lane & 3) >= 2

    def sweep(s):
        for_dirs(lambda d: shell_recv(s, d).wait_recv())
        tile = lambda d: cols_in[s, d - 2].astype(f32)
        side_own = jnp.where(left_lanes, tile(LEFT), tile(RIGHT))
        side_up = jnp.where(left_lanes, tile(UL), tile(UR))
        side_down = jnp.where(left_lanes, tile(DL), tile(DR))
        above = [rows_in[s, 0, i].astype(f32) for i in range(2)]
        below = [rows_in[s, 1, i].astype(f32) for i in range(2)]
        v = {}
        for r in range(axial):
            edge = pltpu.roll(side_own, 4 * r, 1) if r else side_own
            v[r] = jnp.concatenate([mot[s, r], edge], axis=1)
        v[-1] = jnp.concatenate([above[1], pltpu.roll(side_up, 4 * (axial - 1), 1)], axis=1)
        v[axial] = jnp.concatenate([below[0], side_down], axis=1)
        width = circum + 128

        def across(x):
            return pltpu.roll(x, 1, 1) + pltpu.roll(x, width - 1, 1) - 4.0 * x

        moment = {}
        for r in range(-1, axial + 1):
            if r == -1:
                lap = across(v[r])[:, :circum] + above[0] + v[0][:, :circum]
            elif r == axial:
                lap = across(v[r])[:, :circum] + below[1] + v[axial - 1][:, :circum]
            else:
                lap = across(v[r]) + v[r - 1] + v[r + 1]
            moment[r] = kext[r + 1, :, : lap.shape[1]] * lap
        out = []
        for r in range(axial):
            bend = (
                across(moment[r])[:, :circum]
                + moment[r - 1][:, :circum]
                + moment[r + 1][:, :circum]
            )
            here, load = mot[s, r], frc[axial + r]
            bend_re, bend_im = bend[:8], bend[8:]
            v_re, v_im = here[:8], here[8:]
            sh, a, m = coef[0, r], coef[1, r], coef[2, r]
            res_re = load[:8] - (bend_re - loss_factor * bend_im + sh * v_re)
            res_im = load[8:] - (bend_im + loss_factor * bend_re + sh * v_im)
            new = jnp.concatenate(
                [v_re + res_re * a + res_im * m, v_im + res_im * a - res_re * m], axis=0
            )
            mot[s + 1, r] = new
            out.append(new)
        return out

    def round_body(rnd, _):
        b_all(rnd).wait_recv()
        total = None
        for q in range(nb // per):
            block = jnp.concatenate([gb[rnd, q * per + i] for i in range(per)], axis=1)
            term = dot(block, mats[q], ((1,), (1,)))
            total = term if total is None else total + term
        re, im = total[:8], total[8:]
        both = jnp.concatenate(
            [re - pltpu.roll(im, 2 * pd, 1), im + pltpu.roll(re, 2 * pd, 1)], axis=0
        )
        pressure = spread(both)
        press[...] = pressure
        double = spread(pltpu.roll(both, 128 - pd, 1))
        s = SWEEPS * rnd
        neumann = jnp.zeros((16, 128), f32)
        picked = None
        for part in split(mot[s].reshape(axial * 16, circum)):
            term = dot(part, onehot[...], ((1,), (0,)))
            picked = term if picked is None else picked + term
        picked = picked.reshape(axial, 16, 128)
        for r in range(axial):
            neumann = neumann + picked[r] * rowhot[r : r + 1]
        density = 0.5 * dens[...] + neumann - double
        dens[...] = density

        @pl.when(rnd < ITERS - 1)
        def _():
            ga_src[rnd + 1] = density.astype(jnp.bfloat16)
            a_start(rnd + 1)

        weighted = jnp.where(lane < pd, pressure * weight_row, 0.0)
        spots = jnp.concatenate([weighted * rowhot[r : r + 1] for r in range(axial)], axis=0)
        fluid = None
        for part in split(spots):
            term = dot(part, onehot[...], ((1,), (1,)))
            fluid = term if fluid is None else fluid + term
        fluid = fluid.reshape(axial, 16, circum)
        for r in range(axial):
            frc[axial + r] = frc[r] - fluid[r]

        for i in range(SWEEPS):
            rows = sweep(s + i)
            if i < SWEEPS - 1:
                @pl.when(rnd < ITERS - 1)
                def _():
                    a_wait(rnd + 1)
                    b_start(rnd + 1)

                shell_start(s + i + 1, rows)
            else:
                @pl.when(rnd < ITERS - 1)
                def _():
                    shell_start(s + i + 1, rows)
        return 0

    lax.fori_loop(0, ITERS, round_body, 0)

    density_out[...] = dens[...][:, :pd]
    pressure_out[...] = press[...][:, :pd]
    for r in range(axial):
        motion_out[:, r, :] = mot[STEPS, r]

    for j in range(1, nc):
        copy(pa_src, pa.at[j - 1], pan_send.at[j - 1], pan_recv.at[j - 1], me).wait_send()
    pb_all.wait_send()
    for_dirs(lambda d: stiff_copy(d).wait_send() if d in stiff_dirs else None)

    def finish_round(rnd, _):
        for j in range(1, nc):
            copy(ga_src.at[rnd], ga.at[rnd, j - 1], a_send.at[rnd, j - 1], a_recv.at[rnd, j - 1],
                 me).wait_send()
        b_all(rnd).wait_send()
        for i in range(SWEEPS):
            for_dirs(lambda d: shell_copy(SWEEPS * rnd + i, d).wait_send())
        return 0

    lax.fori_loop(0, ITERS, finish_round, 0)


def per_device(nb, nc, panels, node, hoops, density, motion, force, stiffness):
    pd = panels.shape[1]
    channels, axial, circum = motion.shape
    per = math.gcd(nb, 8)
    f32, bf16 = jnp.float32, jnp.bfloat16
    vmem = pl.BlockSpec(memory_space=pltpu.VMEM)
    hbm = pl.BlockSpec(memory_space=pltpu.HBM)
    dma = pltpu.SemaphoreType.DMA
    scratch = [
        pltpu.VMEM((STEPS + 1, axial, channels, circum), f32),
        pltpu.VMEM((2 * axial, channels, circum), f32),
        pltpu.VMEM((STEPS, 2, 2, channels, circum), bf16),
        pltpu.VMEM((STEPS, 2, 2, channels, circum), bf16),
        pltpu.VMEM((STEPS, 6, channels, 128), bf16),
        pltpu.VMEM((STEPS, channels, 128), bf16),
        pltpu.VMEM((4, axial, circum), f32),
        pltpu.VMEM((axial + 2, channels, circum + 128), f32),
        pltpu.VMEM((3, axial, 8, circum), f32),
        pltpu.VMEM((circum, 128), bf16),
        pltpu.VMEM((8, 128), f32),
        pltpu.VMEM((channels, 128), f32),
        pltpu.VMEM((channels, 128), f32),
        pltpu.VMEM((24, 128), f32),
        pltpu.VMEM((ITERS, nc - 1, channels, 128), bf16),
        pltpu.VMEM((ITERS, nb, channels, 128), bf16),
        pltpu.VMEM((ITERS, channels, 128), bf16),
        pltpu.VMEM((nc - 1, 8, 128), f32),
        pltpu.VMEM((nb, 8, 128), f32),
        pltpu.VMEM((8, 128), f32),
        pltpu.VMEM((nb // per, 4 * pd, per * 128), bf16),
        dma((STEPS, 8)), dma((STEPS, 8)), dma((4,)), dma((4,)),
        dma((ITERS, nc - 1)), dma((ITERS, nc - 1)), dma((ITERS,)), dma((ITERS,)),
        dma((nc,)), dma((nc,)),
        pltpu.VMEM(panels.shape, f32), pltpu.SMEM(node.shape, jnp.int32),
        pltpu.SMEM(hoops.shape, jnp.int32), pltpu.VMEM(density.shape, f32),
        pltpu.VMEM(motion.shape, f32), pltpu.VMEM(force.shape, f32),
        pltpu.VMEM(stiffness.shape, f32), dma((7,)),
    ]
    return pl.pallas_call(
        functools.partial(kernel, nb, nc, pd),
        out_shape=(
            jax.ShapeDtypeStruct(density.shape, f32),
            jax.ShapeDtypeStruct(density.shape, f32),
            jax.ShapeDtypeStruct(motion.shape, f32),
        ),
        in_specs=[hbm] * 7,
        out_specs=(vmem, vmem, vmem),
        scratch_shapes=scratch,
        compiler_params=pltpu.CompilerParams(
            collective_id=0, has_side_effects=True, vmem_limit_bytes=64 * 1024 * 1024
        ),
    )(panels, node, hoops, density, motion, force, stiffness)


def solution(mesh):
    nb, nc = mesh.shape["blk"], mesh.shape["circ"]
    in_specs = (
        P(None, ("blk", "circ")),
        P(("blk", "circ")),
        P(),
        P(None, ("blk", "circ")),
        P(None, "blk", "circ"),
        P(None, "blk", "circ"),
        P("blk", "circ"),
    )
    out_specs = (P(None, ("blk", "circ")), P(None, ("blk", "circ")), P(None, "blk", "circ"))
    return jax.shard_map(
        functools.partial(per_device, nb, nc),
        mesh=mesh, in_specs=in_specs, out_specs=out_specs, check_vma=False,
    )
```

```python
import functools
import math

import jax
import jax.numpy as jnp
from jax import lax
from jax.experimental import pallas as pl
from jax.experimental.pallas import tpu as pltpu
from jax.sharding import PartitionSpec as P

MESH = pl.DeviceIdType.MESH
ITERS = 4
SWEEPS = 2
STEPS = ITERS * SWEEPS

wave_number = 4.0
single_scale = 30.0
double_scale = 6.0
hoop_spring = 40.0
inertia_term = 4.0
loss_factor = 0.2
relaxation = 0.3

COS = (
    0.9999999890590228, -19.739204499454, 64.93911745989914, -85.45013953093448,
    60.16763095128989, -25.96759924954187, 6.528658162606979,
)
SIN = (
    6.283185302511502, -41.34170040531754, 81.6051313857969, -76.70301535383193,
    42.02592698564183, -14.899846667160109, 3.2381375090822355,
)

UP, DOWN, LEFT, RIGHT, UL, UR, DL, DR = range(8)
OPPOSITE = {UP: DOWN, DOWN: UP, LEFT: RIGHT, RIGHT: LEFT, UL: DR, UR: DL, DL: UR, DR: UL}


def poly(coefs, x):
    acc = jnp.full_like(x, coefs[-1])
    for c in coefs[-2::-1]:
        acc = acc * x + c
    return acc


def split(x):
    high = x.astype(jnp.bfloat16)
    low = (x - high.astype(jnp.float32)).astype(jnp.bfloat16)
    return high, low


def dot(a, b, dims):
    return lax.dot_general(a, b, (dims, ((), ())), preferred_element_type=jnp.float32)


def kernel(
    nb, nc, pd,
    panels_hbm, node_hbm, hoops_hbm, density_hbm, motion_hbm, force_hbm, stiff_hbm,
    density_out, pressure_out, motion_out,
    mot, frc, rows_own, rows_in, cols_in, cols_own, stiff_in, kext, coef, onehot, rowhot,
    dens, press, wide, ga, gb, ga_src, pa, pb, pa_src, mats,
    sh_send, sh_recv, st_send, st_recv, a_send, a_recv, b_send, b_recv, pan_send, pan_recv,
    panels, node, hoops, density_in, motion_in, force_in, stiff, in_sems,
):
    f32 = jnp.float32
    b = lax.axis_index("blk")
    c = lax.axis_index("circ")
    axial, circum = stiff.shape
    last_tile = circum - 128
    cleft, cright = lax.rem(c + nc - 1, nc), lax.rem(c + 1, nc)
    where_to = {
        UP: (b - 1, c), DOWN: (b + 1, c), LEFT: (b, cleft), RIGHT: (b, cright),
        UL: (b - 1, cleft), UR: (b - 1, cright), DL: (b + 1, cleft), DR: (b + 1, cright),
    }
    has_up, has_down = b > 0, b < nb - 1

    def for_far(fn):
        @pl.when(has_up)
        def _():
            for d in (UP, UL, UR):
                fn(d)

        @pl.when(has_down)
        def _():
            for d in (DOWN, DL, DR):
                fn(d)

    def for_dirs(fn):
        for_far(fn)
        fn(LEFT)
        fn(RIGHT)

    def for_peers(fn):
        if nb <= 8:
            for j in range(1, nb):
                fn(lax.rem(b + j, nb))
        else:
            def body(j, _):
                fn(lax.rem(b + j, nb))
                return 0

            lax.fori_loop(1, nb, body, 0)

    loads = [
        pltpu.make_async_copy(src, dst, in_sems.at[n])
        for n, (src, dst) in enumerate((
            (panels_hbm, panels), (density_hbm, density_in), (motion_hbm, motion_in),
            (stiff_hbm, stiff), (force_hbm, force_in), (node_hbm, node), (hoops_hbm, hoops),
        ))
    ]
    for load in loads:
        load.start()

    @pl.when(jnp.logical_not(has_up))
    def _():
        rows_in[:, 0] = jnp.zeros_like(rows_in[:, 0])
        cols_in[:, UL - 2] = jnp.zeros_like(cols_in[:, UL - 2])
        cols_in[:, UR - 2] = jnp.zeros_like(cols_in[:, UR - 2])
        stiff_in[UP] = jnp.zeros_like(stiff_in[UP])

    @pl.when(jnp.logical_not(has_down))
    def _():
        rows_in[:, 1] = jnp.zeros_like(rows_in[:, 1])
        cols_in[:, DL - 2] = jnp.zeros_like(cols_in[:, DL - 2])
        cols_in[:, DR - 2] = jnp.zeros_like(cols_in[:, DR - 2])
        stiff_in[DOWN] = jnp.zeros_like(stiff_in[DOWN])

    barrier = pltpu.get_barrier_semaphore()

    def greet(device):
        pl.semaphore_signal(barrier, inc=1, device_id=device, device_id_type=MESH)

    for j in range(1, nc):
        greet((b, lax.rem(c + j, nc)))
    for_peers(lambda peer: greet((peer, c)))

    @pl.when(has_up)
    def _():
        greet(where_to[UL])
        greet(where_to[UR])

    @pl.when(has_down)
    def _():
        greet(where_to[DL])
        greet(where_to[DR])

    lane = lax.broadcasted_iota(jnp.int32, (16, 128), 1)
    lane8 = lane[:8]

    def spread(x):
        x = jnp.where(lane[: x.shape[0]] < pd, x, 0.0)
        step = pd
        while step < 128:
            x = x + pltpu.roll(x, step, 1)
            step *= 2
        return x

    wide[...] = jnp.zeros_like(wide)
    loads[0].wait()
    loads[1].wait()
    wide[0:4, 0:pd] = panels[...]
    wide[8:24, 0:pd] = density_in[...]
    own = spread(wide[0:8, :])
    dens[...] = spread(wide[8:24, :])
    pa_src[...] = own
    ga_src[0] = dens[...].astype(jnp.bfloat16)

    pl.semaphore_wait(
        barrier,
        (nc - 1) + (nb - 1) + 2 * has_up.astype(jnp.int32) + 2 * has_down.astype(jnp.int32),
    )

    def copy(src, dst, send, recv, device):
        return pltpu.make_async_remote_copy(
            src_ref=src, dst_ref=dst, send_sem=send, recv_sem=recv,
            device_id=device, device_id_type=MESH,
        )

    me = (b, c)

    def a_start(rnd):
        for j in range(1, nc):
            copy(ga_src.at[rnd], ga.at[rnd, j - 1], a_send.at[rnd, j - 1], a_recv.at[rnd, j - 1],
                 (b, lax.rem(c + j, nc))).start()

    def a_wait(rnd):
        for j in range(1, nc):
            copy(ga_src.at[rnd], ga.at[rnd, j - 1], a_send.at[rnd, j - 1], a_recv.at[rnd, j - 1],
                 me).wait_recv()

    def merge(own_block, parts):
        group = lane[: own_block.shape[0]] // pd
        out = own_block
        for j in range(1, nc):
            out = jnp.where(group == lax.rem(c + nc - j, nc), parts[j - 1], out)
        return out

    def b_start(rnd):
        parts = [ga[rnd, j].astype(f32) for j in range(nc - 1)]
        gb[rnd, b] = merge(ga_src[rnd].astype(f32), parts).astype(jnp.bfloat16)
        for_peers(lambda peer: copy(gb.at[rnd, b], gb.at[rnd, b], b_send.at[rnd], b_recv.at[rnd],
                                    (peer, c)).start())

    def b_all(rnd):
        part = gb.at[rnd, pl.ds(0, nb - 1)]
        return copy(part, part, b_send.at[rnd], b_recv.at[rnd], me)

    for j in range(1, nc):
        copy(pa_src, pa.at[j - 1], pan_send.at[j - 1], pan_recv.at[j - 1],
             (b, lax.rem(c + j, nc))).start()
    a_start(0)
    loads[3].wait()
    stiff_dirs = (UP, DOWN, LEFT, RIGHT)

    def stiff_copy(d):
        return copy(stiff, stiff_in.at[OPPOSITE[d]], st_send.at[d], st_recv.at[OPPOSITE[d]],
                    where_to[d])

    for_dirs(lambda d: stiff_copy(d).start() if d in stiff_dirs else None)

    def shell_copy(s, d):
        o = OPPOSITE[d]
        if d in (UP, DOWN):
            src = rows_own.at[s, 0 if d == UP else 1]
            dst = rows_in.at[s, 0 if o == UP else 1]
        else:
            src, dst = cols_own.at[s], cols_in.at[s, o - 2]
        return copy(src, dst, sh_send.at[s, d], sh_recv.at[s, o], where_to[d])

    def shell_recv(s, d):
        if d in (UP, DOWN):
            dst = rows_in.at[s, 0 if d == UP else 1]
        else:
            dst = cols_in.at[s, d - 2]
        return copy(dst, dst, sh_send.at[s, d], sh_recv.at[s, d], me)

    place = (lane + 2) & 127
    row_of = ((128 - (place - (place & 3))) & 127) // 4

    def shell_start(s, rows):
        packed = None
        for r in range(axial):
            edge = jnp.where(lane < 64, rows[r][:, :128], rows[r][:, last_tile:])
            edge = pltpu.roll(edge, (128 - 4 * r) % 128, 1) if r else edge
            packed = edge if r == 0 else jnp.where(row_of == r, edge, packed)
        bf = jnp.bfloat16
        cols_own[s] = packed.astype(bf)
        for n, at in enumerate((0, axial - 2)):
            for i in range(2):
                rows_own[s, n, i] = rows[at + i].astype(bf)
        for_dirs(lambda d: shell_copy(s, d).start())

    loads[2].wait()
    first = []
    for r in range(axial):
        row = motion_in[:, r, :]
        mot[0, r] = row
        first.append(row)
    shell_start(0, first)
    for load in loads[4:]:
        load.wait()
    for r in range(axial):
        frc[r] = force_in[:, r, :]

    sub = lax.broadcasted_iota(jnp.int32, (axial, circum), 0) + b * axial
    hoop = jnp.zeros((axial, circum), f32)
    for h in range(hoops.shape[0]):
        hoop = jnp.where(sub == hoops[h], 1.0, hoop)
    k = stiff[...]
    shift = hoop_spring * hoop - inertia_term
    diag_re = 20.0 * k + shift
    diag_im = (20.0 * loss_factor) * k
    scale = relaxation / (diag_re * diag_re + diag_im * diag_im)
    inv_re, inv_im = diag_re * scale, diag_im * scale
    for r in range(axial):
        for n, x in enumerate((shift, inv_re, inv_im)):
            coef[n, r] = jnp.broadcast_to(x[r : r + 1], (8, circum))

    nodes = jnp.zeros((8, 128), jnp.int32)
    for p in range(pd):
        nodes = jnp.where((lane8 & (pd - 1)) == p, node[p], nodes)
    node_row = nodes // circum
    node_col = nodes - node_row * circum
    rowhot[...] = (node_row == lax.broadcasted_iota(jnp.int32, (8, 128), 0)).astype(f32)
    col_iota = lax.broadcasted_iota(jnp.int32, (circum, 128), 0)
    onehot[...] = (
        (jnp.broadcast_to(node_col[0:1], (circum, 128)) == col_iota).astype(f32).astype(jnp.bfloat16)
    )

    for j in range(1, nc):
        copy(pa_src, pa.at[j - 1], pan_send.at[j - 1], pan_recv.at[j - 1], me).wait_recv()
    a_wait(0)
    pb[b] = merge(pa_src[...], [pa[j] for j in range(nc - 1)])
    for_peers(lambda peer: copy(pb.at[b], pb.at[b], pan_send.at[nc - 1], pan_recv.at[nc - 1],
                                (peer, c)).start())
    b_start(0)
    pb_part = pb.at[pl.ds(0, nb - 1)]
    pb_all = copy(pb_part, pb_part, pan_send.at[nc - 1], pan_recv.at[nc - 1], me)

    for_dirs(
        lambda d: copy(stiff_in.at[d], stiff_in.at[d], st_send.at[d], st_recv.at[d], me).wait_recv()
        if d in stiff_dirs else None
    )
    right_tile = stiff_in[RIGHT][:, :128]
    left_tile = stiff_in[LEFT][:, last_tile:]
    side = jnp.where(lane8 < 64, right_tile, left_tile)
    k_up, k_down = stiff_in[UP], stiff_in[DOWN]
    for r in range(axial + 2):
        if r == 0:
            line = k_up[axial - 1 : axial]
        elif r == axial + 1:
            line = k_down[0:1]
        else:
            line = k[r - 1 : r]
            kext[r, :, circum:] = jnp.broadcast_to(side[r - 1 : r], (16, 128))
        kext[r, :, :circum] = jnp.broadcast_to(line, (16, circum))

    radial = jnp.sqrt(own[0:1] * own[0:1] + own[1:2] * own[1:2])
    eye = lax.broadcasted_iota(jnp.int32, (pd, 128), 0) == lax.broadcasted_iota(
        jnp.int32, (pd, 128), 1
    )

    def column(line):
        return jnp.sum(jnp.where(eye, jnp.broadcast_to(line, (pd, 128)), 0.0), axis=1, keepdims=True)

    tx, ty, tz = column(own[0:1]), column(own[1:2]), column(own[2:3])
    nx, ny = column(own[0:1] / radial), column(own[1:2] / radial)
    weight_row = own[3:4] * (pd * nb * nc / (8.0 * math.pi))

    pb_all.wait_recv()

    per = mats.shape[2] // 128
    for q in range(nb // per):
        for i in range(per):
            src = pb[q * per + i]
            dx, dy, dz = tx - src[0:1], ty - src[1:2], tz - src[2:3]
            area = src[3:4]
            dist_sq = dx * dx + dy * dy + dz * dz + area * (1.0 / math.pi)
            inverse = lax.rsqrt(dist_sq)
            phase = (wave_number * dist_sq) * inverse
            turns = phase * (1.0 / (2.0 * math.pi))
            turns = turns - jnp.round(turns)
            sq = turns * turns
            cosine = poly(COS, sq)
            sine = poly(SIN, sq) * turns
            weight = area * (1.0 / (4.0 * math.pi)) * inverse
            single = single_scale * weight
            double = double_scale * weight * (nx * dx + ny * dy) * inverse * inverse
            at = pl.ds(i * 128, 128)
            bf = jnp.bfloat16
            mats[q, 0:pd, at] = (single * cosine).astype(bf)
            mats[q, pd : 2 * pd, at] = (double * (-cosine - phase * sine)).astype(bf)
            mats[q, 2 * pd : 3 * pd, at] = (single * sine).astype(bf)
            mats[q, 3 * pd : 4 * pd, at] = (double * (phase * cosine - sine)).astype(bf)

    left_lanes = (lane & 3) >= 2

    def sweep(s):
        tile = lambda d: cols_in[s, d - 2].astype(f32)
        width = circum + 128
        v, moment, out = {}, {}, {}

        def across(x):
            return pltpu.roll(x, 1, 1) + pltpu.roll(x, width - 1, 1) - 4.0 * x

        def bending(r, lap):
            moment[r] = kext[r + 1, :, : lap.shape[1]] * lap

        def update(r):
            bend = (
                across(moment[r])[:, :circum]
                + moment[r - 1][:, :circum]
                + moment[r + 1][:, :circum]
            )
            here, load = mot[s, r], frc[axial + r]
            bend_re, bend_im = bend[:8], bend[8:]
            v_re, v_im = here[:8], here[8:]
            sh, a, m = coef[0, r], coef[1, r], coef[2, r]
            res_re = load[:8] - (bend_re - loss_factor * bend_im + sh * v_re)
            res_im = load[8:] - (bend_im + loss_factor * bend_re + sh * v_im)
            new = jnp.concatenate(
                [v_re + res_re * a + res_im * m, v_im + res_im * a - res_re * m], axis=0
            )
            mot[s + 1, r] = new
            out[r] = new

        shell_recv(s, LEFT).wait_recv()
        shell_recv(s, RIGHT).wait_recv()
        side_own = jnp.where(left_lanes, tile(LEFT), tile(RIGHT))
        for r in range(axial):
            edge = pltpu.roll(side_own, 4 * r, 1) if r else side_own
            v[r] = jnp.concatenate([mot[s, r], edge], axis=1)
        for r in range(1, axial - 1):
            bending(r, across(v[r]) + v[r - 1] + v[r + 1])
        for r in range(2, axial - 2):
            update(r)

        for_far(lambda d: shell_recv(s, d).wait_recv())
        side_up = jnp.where(left_lanes, tile(UL), tile(UR))
        side_down = jnp.where(left_lanes, tile(DL), tile(DR))
        above = [rows_in[s, 0, i].astype(f32) for i in range(2)]
        below = [rows_in[s, 1, i].astype(f32) for i in range(2)]
        v[-1] = jnp.concatenate([above[1], pltpu.roll(side_up, 4 * (axial - 1), 1)], axis=1)
        v[axial] = jnp.concatenate([below[0], side_down], axis=1)
        bending(-1, across(v[-1])[:, :circum] + above[0] + v[0][:, :circum])
        bending(axial, across(v[axial])[:, :circum] + below[1] + v[axial - 1][:, :circum])
        for r in (0, axial - 1):
            bending(r, across(v[r]) + v[r - 1] + v[r + 1])
        for r in (0, 1, axial - 2, axial - 1):
            update(r)
        return [out[r] for r in range(axial)]

    def round_body(rnd, _):
        b_all(rnd).wait_recv()
        total = None
        for q in range(nb // per):
            block = jnp.concatenate([gb[rnd, q * per + i] for i in range(per)], axis=1)
            term = dot(block, mats[q], ((1,), (1,)))
            total = term if total is None else total + term
        re, im = total[:8], total[8:]
        both = jnp.concatenate(
            [re - pltpu.roll(im, 2 * pd, 1), im + pltpu.roll(re, 2 * pd, 1)], axis=0
        )
        pressure = spread(both)
        press[...] = pressure
        double = spread(pltpu.roll(both, 128 - pd, 1))
        s = SWEEPS * rnd
        neumann = jnp.zeros((16, 128), f32)
        picked = None
        for part in split(mot[s].reshape(axial * 16, circum)):
            term = dot(part, onehot[...], ((1,), (0,)))
            picked = term if picked is None else picked + term
        picked = picked.reshape(axial, 16, 128)
        for r in range(axial):
            neumann = neumann + picked[r] * rowhot[r : r + 1]
        density = 0.5 * dens[...] + neumann - double
        dens[...] = density

        @pl.when(rnd < ITERS - 1)
        def _():
            ga_src[rnd + 1] = density.astype(jnp.bfloat16)
            a_start(rnd + 1)

        weighted = jnp.where(lane < pd, pressure * weight_row, 0.0)
        spots = jnp.concatenate([weighted * rowhot[r : r + 1] for r in range(axial)], axis=0)
        fluid = None
        for part in split(spots):
            term = dot(part, onehot[...], ((1,), (1,)))
            fluid = term if fluid is None else fluid + term
        fluid = fluid.reshape(axial, 16, circum)
        for r in range(axial):
            frc[axial + r] = frc[r] - fluid[r]

        for i in range(SWEEPS):
            rows = sweep(s + i)
            if i < SWEEPS - 1:
                shell_start(s + i + 1, rows)

                @pl.when(rnd < ITERS - 1)
                def _():
                    a_wait(rnd + 1)
                    b_start(rnd + 1)
            else:
                @pl.when(rnd < ITERS - 1)
                def _():
                    shell_start(s + i + 1, rows)
        return 0

    lax.fori_loop(0, ITERS, round_body, 0)

    density_out[...] = dens[...][:, :pd]
    pressure_out[...] = press[...][:, :pd]
    for r in range(axial):
        motion_out[:, r, :] = mot[STEPS, r]

    for j in range(1, nc):
        copy(pa_src, pa.at[j - 1], pan_send.at[j - 1], pan_recv.at[j - 1], me).wait_send()
    pb_all.wait_send()
    for_dirs(lambda d: stiff_copy(d).wait_send() if d in stiff_dirs else None)

    def finish_round(rnd, _):
        for j in range(1, nc):
            copy(ga_src.at[rnd], ga.at[rnd, j - 1], a_send.at[rnd, j - 1], a_recv.at[rnd, j - 1],
                 me).wait_send()
        b_all(rnd).wait_send()
        for i in range(SWEEPS):
            for_dirs(lambda d: shell_copy(SWEEPS * rnd + i, d).wait_send())
        return 0

    lax.fori_loop(0, ITERS, finish_round, 0)


def per_device(nb, nc, panels, node, hoops, density, motion, force, stiffness):
    pd = panels.shape[1]
    channels, axial, circum = motion.shape
    per = math.gcd(nb, 8)
    f32, bf16 = jnp.float32, jnp.bfloat16
    vmem = pl.BlockSpec(memory_space=pltpu.VMEM)
    hbm = pl.BlockSpec(memory_space=pltpu.HBM)
    dma = pltpu.SemaphoreType.DMA
    scratch = [
        pltpu.VMEM((STEPS + 1, axial, channels, circum), f32),
        pltpu.VMEM((2 * axial, channels, circum), f32),
        pltpu.VMEM((STEPS, 2, 2, channels, circum), bf16),
        pltpu.VMEM((STEPS, 2, 2, channels, circum), bf16),
        pltpu.VMEM((STEPS, 6, channels, 128), bf16),
        pltpu.VMEM((STEPS, channels, 128), bf16),
        pltpu.VMEM((4, axial, circum), f32),
        pltpu.VMEM((axial + 2, channels, circum + 128), f32),
        pltpu.VMEM((3, axial, 8, circum), f32),
        pltpu.VMEM((circum, 128), bf16),
        pltpu.VMEM((8, 128), f32),
        pltpu.VMEM((channels, 128), f32),
        pltpu.VMEM((channels, 128), f32),
        pltpu.VMEM((24, 128), f32),
        pltpu.VMEM((ITERS, nc - 1, channels, 128), bf16),
        pltpu.VMEM((ITERS, nb, channels, 128), bf16),
        pltpu.VMEM((ITERS, channels, 128), bf16),
        pltpu.VMEM((nc - 1, 8, 128), f32),
        pltpu.VMEM((nb, 8, 128), f32),
        pltpu.VMEM((8, 128), f32),
        pltpu.VMEM((nb // per, 4 * pd, per * 128), bf16),
        dma((STEPS, 8)), dma((STEPS, 8)), dma((4,)), dma((4,)),
        dma((ITERS, nc - 1)), dma((ITERS, nc - 1)), dma((ITERS,)), dma((ITERS,)),
        dma((nc,)), dma((nc,)),
        pltpu.VMEM(panels.shape, f32), pltpu.SMEM(node.shape, jnp.int32),
        pltpu.SMEM(hoops.shape, jnp.int32), pltpu.VMEM(density.shape, f32),
        pltpu.VMEM(motion.shape, f32), pltpu.VMEM(force.shape, f32),
        pltpu.VMEM(stiffness.shape, f32), dma((7,)),
    ]
    return pl.pallas_call(
        functools.partial(kernel, nb, nc, pd),
        out_shape=(
            jax.ShapeDtypeStruct(density.shape, f32),
            jax.ShapeDtypeStruct(density.shape, f32),
            jax.ShapeDtypeStruct(motion.shape, f32),
        ),
        in_specs=[hbm] * 7,
        out_specs=(vmem, vmem, vmem),
        scratch_shapes=scratch,
        compiler_params=pltpu.CompilerParams(
            collective_id=0, has_side_effects=True, vmem_limit_bytes=64 * 1024 * 1024
        ),
    )(panels, node, hoops, density, motion, force, stiffness)


def solution(mesh):
    nb, nc = mesh.shape["blk"], mesh.shape["circ"]
    in_specs = (
        P(None, ("blk", "circ")),
        P(("blk", "circ")),
        P(),
        P(None, ("blk", "circ")),
        P(None, "blk", "circ"),
        P(None, "blk", "circ"),
        P("blk", "circ"),
    )
    out_specs = (P(None, ("blk", "circ")), P(None, ("blk", "circ")), P(None, "blk", "circ"))
    return jax.shard_map(
        functools.partial(per_device, nb, nc),
        mesh=mesh, in_specs=in_specs, out_specs=out_specs, check_vma=False,
    )
```

```python
import functools
import math

import jax
import jax.numpy as jnp
from jax import lax
from jax.experimental import pallas as pl
from jax.experimental.pallas import tpu as pltpu
from jax.sharding import PartitionSpec as P

MESH = pl.DeviceIdType.MESH
ITERS = 4
SWEEPS = 2
STEPS = ITERS * SWEEPS

wave_number = 4.0
single_scale = 30.0
double_scale = 6.0
hoop_spring = 40.0
inertia_term = 4.0
loss_factor = 0.2
relaxation = 0.3

COS = (
    0.9999999890590228, -19.739204499454, 64.93911745989914, -85.45013953093448,
    60.16763095128989, -25.96759924954187, 6.528658162606979,
)
SIN = (
    6.283185302511502, -41.34170040531754, 81.6051313857969, -76.70301535383193,
    42.02592698564183, -14.899846667160109, 3.2381375090822355,
)

UP, DOWN, LEFT, RIGHT, UL, UR, DL, DR = range(8)
OPPOSITE = {UP: DOWN, DOWN: UP, LEFT: RIGHT, RIGHT: LEFT, UL: DR, UR: DL, DL: UR, DR: UL}


def poly(coefs, x):
    acc = jnp.full_like(x, coefs[-1])
    for c in coefs[-2::-1]:
        acc = acc * x + c
    return acc


def split(x):
    high = x.astype(jnp.bfloat16)
    low = (x - high.astype(jnp.float32)).astype(jnp.bfloat16)
    return high, low


def dot(a, b, dims):
    return lax.dot_general(a, b, (dims, ((), ())), preferred_element_type=jnp.float32)


def kernel(
    nb, nc, pd,
    panels_hbm, node_hbm, hoops_hbm, density_hbm, motion_hbm, force_hbm, stiff_hbm,
    density_out, pressure_out, motion_out,
    mot, frc, rows_own, rows_in, cols_in, cols_own, stiff_in, kext, coef, onehot, rowhot,
    dens, held, press, wide, ga, gb, ga_src, pa, pb, pa_src, mats,
    sh_send, sh_recv, st_send, st_recv, a_send, a_recv, b_send, b_recv, pan_send, pan_recv,
    panels, node, hoops, density_in, motion_in, force_in, stiff, in_sems,
):
    f32 = jnp.float32
    b = lax.axis_index("blk")
    c = lax.axis_index("circ")
    axial, circum = stiff.shape
    last_tile = circum - 128
    cleft, cright = lax.rem(c + nc - 1, nc), lax.rem(c + 1, nc)
    where_to = {
        UP: (b - 1, c), DOWN: (b + 1, c), LEFT: (b, cleft), RIGHT: (b, cright),
        UL: (b - 1, cleft), UR: (b - 1, cright), DL: (b + 1, cleft), DR: (b + 1, cright),
    }
    has_up, has_down = b > 0, b < nb - 1

    def for_far(fn):
        @pl.when(has_up)
        def _():
            for d in (UP, UL, UR):
                fn(d)

        @pl.when(has_down)
        def _():
            for d in (DOWN, DL, DR):
                fn(d)

    def for_dirs(fn):
        for_far(fn)
        fn(LEFT)
        fn(RIGHT)

    def for_peers(fn):
        if nb <= 8:
            for j in range(1, nb):
                fn(lax.rem(b + j, nb))
        else:
            def body(j, _):
                fn(lax.rem(b + j, nb))
                return 0

            lax.fori_loop(1, nb, body, 0)

    loads = [
        pltpu.make_async_copy(src, dst, in_sems.at[n])
        for n, (src, dst) in enumerate((
            (panels_hbm, panels), (density_hbm, density_in), (motion_hbm, motion_in),
            (stiff_hbm, stiff), (force_hbm, force_in), (node_hbm, node), (hoops_hbm, hoops),
        ))
    ]
    for load in loads:
        load.start()

    @pl.when(jnp.logical_not(has_up))
    def _():
        rows_in[:, 0] = jnp.zeros_like(rows_in[:, 0])
        cols_in[:, UL - 2] = jnp.zeros_like(cols_in[:, UL - 2])
        cols_in[:, UR - 2] = jnp.zeros_like(cols_in[:, UR - 2])
        stiff_in[UP] = jnp.zeros_like(stiff_in[UP])

    @pl.when(jnp.logical_not(has_down))
    def _():
        rows_in[:, 1] = jnp.zeros_like(rows_in[:, 1])
        cols_in[:, DL - 2] = jnp.zeros_like(cols_in[:, DL - 2])
        cols_in[:, DR - 2] = jnp.zeros_like(cols_in[:, DR - 2])
        stiff_in[DOWN] = jnp.zeros_like(stiff_in[DOWN])

    barrier = pltpu.get_barrier_semaphore()

    def greet(device):
        pl.semaphore_signal(barrier, inc=1, device_id=device, device_id_type=MESH)

    for j in range(1, nc):
        greet((b, lax.rem(c + j, nc)))
    for_peers(lambda peer: greet((peer, c)))

    @pl.when(has_up)
    def _():
        greet(where_to[UL])
        greet(where_to[UR])

    @pl.when(has_down)
    def _():
        greet(where_to[DL])
        greet(where_to[DR])

    lane = lax.broadcasted_iota(jnp.int32, (16, 128), 1)
    lane8 = lane[:8]

    def spread(x):
        x = jnp.where(lane[: x.shape[0]] < pd, x, 0.0)
        step = pd
        while step < 128:
            x = x + pltpu.roll(x, step, 1)
            step *= 2
        return x

    wide[...] = jnp.zeros_like(wide)
    loads[0].wait()
    loads[1].wait()
    wide[0:4, 0:pd] = panels[...]
    wide[8:24, 0:pd] = density_in[...]
    own = spread(wide[0:8, :])
    dens[...] = spread(wide[8:24, :])
    pa_src[...] = own
    ga_src[0] = dens[...].astype(jnp.bfloat16)

    pl.semaphore_wait(
        barrier,
        (nc - 1) + (nb - 1) + 2 * has_up.astype(jnp.int32) + 2 * has_down.astype(jnp.int32),
    )

    def copy(src, dst, send, recv, device):
        return pltpu.make_async_remote_copy(
            src_ref=src, dst_ref=dst, send_sem=send, recv_sem=recv,
            device_id=device, device_id_type=MESH,
        )

    me = (b, c)

    def a_start(rnd):
        for j in range(1, nc):
            copy(ga_src.at[rnd], ga.at[rnd, j - 1], a_send.at[rnd, j - 1], a_recv.at[rnd, j - 1],
                 (b, lax.rem(c + j, nc))).start()

    def a_wait(rnd):
        for j in range(1, nc):
            copy(ga_src.at[rnd], ga.at[rnd, j - 1], a_send.at[rnd, j - 1], a_recv.at[rnd, j - 1],
                 me).wait_recv()

    def merge(own_block, parts):
        group = lane[: own_block.shape[0]] // pd
        out = own_block
        for j in range(1, nc):
            out = jnp.where(group == lax.rem(c + nc - j, nc), parts[j - 1], out)
        return out

    def b_start(rnd):
        parts = [ga[rnd, j].astype(f32) for j in range(nc - 1)]
        gb[rnd, b] = merge(ga_src[rnd].astype(f32), parts).astype(jnp.bfloat16)
        for_peers(lambda peer: copy(gb.at[rnd, b], gb.at[rnd, b], b_send.at[rnd], b_recv.at[rnd],
                                    (peer, c)).start())

    def b_all(rnd):
        part = gb.at[rnd, pl.ds(0, nb - 1)]
        return copy(part, part, b_send.at[rnd], b_recv.at[rnd], me)

    for j in range(1, nc):
        copy(pa_src, pa.at[j - 1], pan_send.at[j - 1], pan_recv.at[j - 1],
             (b, lax.rem(c + j, nc))).start()
    a_start(0)
    loads[3].wait()
    stiff_dirs = (UP, DOWN, LEFT, RIGHT)

    def stiff_copy(d):
        return copy(stiff, stiff_in.at[OPPOSITE[d]], st_send.at[d], st_recv.at[OPPOSITE[d]],
                    where_to[d])

    for_dirs(lambda d: stiff_copy(d).start() if d in stiff_dirs else None)

    def shell_copy(s, d):
        o = OPPOSITE[d]
        if d in (UP, DOWN):
            src = rows_own.at[s, 0 if d == UP else 1]
            dst = rows_in.at[s, 0 if o == UP else 1]
        else:
            src, dst = cols_own.at[s], cols_in.at[s, o - 2]
        return copy(src, dst, sh_send.at[s, d], sh_recv.at[s, o], where_to[d])

    def shell_recv(s, d):
        if d in (UP, DOWN):
            dst = rows_in.at[s, 0 if d == UP else 1]
        else:
            dst = cols_in.at[s, d - 2]
        return copy(dst, dst, sh_send.at[s, d], sh_recv.at[s, d], me)

    place = (lane + 2) & 127
    row_of = ((128 - (place - (place & 3))) & 127) // 4

    def shell_start(s, rows):
        packed = None
        for r in range(axial):
            edge = jnp.where(lane < 64, rows[r][:, :128], rows[r][:, last_tile:])
            edge = pltpu.roll(edge, (128 - 4 * r) % 128, 1) if r else edge
            packed = edge if r == 0 else jnp.where(row_of == r, edge, packed)
        bf = jnp.bfloat16
        cols_own[s] = packed.astype(bf)
        for n, at in enumerate((0, axial - 2)):
            for i in range(2):
                rows_own[s, n, i] = rows[at + i].astype(bf)
        for_dirs(lambda d: shell_copy(s, d).start())

    loads[2].wait()
    first = []
    for r in range(axial):
        row = motion_in[:, r, :]
        mot[0, r] = row
        first.append(row)
    shell_start(0, first)
    for load in loads[4:]:
        load.wait()
    for r in range(axial):
        frc[r] = force_in[:, r, :]

    sub = lax.broadcasted_iota(jnp.int32, (axial, circum), 0) + b * axial
    hoop = jnp.zeros((axial, circum), f32)
    for h in range(hoops.shape[0]):
        hoop = jnp.where(sub == hoops[h], 1.0, hoop)
    k = stiff[...]
    shift = hoop_spring * hoop - inertia_term
    diag_re = 20.0 * k + shift
    diag_im = (20.0 * loss_factor) * k
    scale = relaxation / (diag_re * diag_re + diag_im * diag_im)
    inv_re, inv_im = diag_re * scale, diag_im * scale
    for r in range(axial):
        for n, x in enumerate((shift, inv_re, inv_im)):
            coef[n, r] = jnp.broadcast_to(x[r : r + 1], (8, circum))

    nodes = jnp.zeros((8, 128), jnp.int32)
    for p in range(pd):
        nodes = jnp.where((lane8 & (pd - 1)) == p, node[p], nodes)
    node_row = nodes // circum
    node_col = nodes - node_row * circum
    rowhot[...] = (node_row == lax.broadcasted_iota(jnp.int32, (8, 128), 0)).astype(f32)
    col_iota = lax.broadcasted_iota(jnp.int32, (circum, 128), 0)
    onehot[...] = (
        (jnp.broadcast_to(node_col[0:1], (circum, 128)) == col_iota).astype(f32).astype(jnp.bfloat16)
    )

    for j in range(1, nc):
        copy(pa_src, pa.at[j - 1], pan_send.at[j - 1], pan_recv.at[j - 1], me).wait_recv()
    a_wait(0)
    pb[b] = merge(pa_src[...], [pa[j] for j in range(nc - 1)])
    for_peers(lambda peer: copy(pb.at[b], pb.at[b], pan_send.at[nc - 1], pan_recv.at[nc - 1],
                                (peer, c)).start())
    b_start(0)
    pb_part = pb.at[pl.ds(0, nb - 1)]
    pb_all = copy(pb_part, pb_part, pan_send.at[nc - 1], pan_recv.at[nc - 1], me)

    for_dirs(
        lambda d: copy(stiff_in.at[d], stiff_in.at[d], st_send.at[d], st_recv.at[d], me).wait_recv()
        if d in stiff_dirs else None
    )
    right_tile = stiff_in[RIGHT][:, :128]
    left_tile = stiff_in[LEFT][:, last_tile:]
    side = jnp.where(lane8 < 64, right_tile, left_tile)
    k_up, k_down = stiff_in[UP], stiff_in[DOWN]
    for r in range(axial + 2):
        if r == 0:
            line = k_up[axial - 1 : axial]
        elif r == axial + 1:
            line = k_down[0:1]
        else:
            line = k[r - 1 : r]
            kext[r, :, circum:] = jnp.broadcast_to(side[r - 1 : r], (16, 128))
        kext[r, :, :circum] = jnp.broadcast_to(line, (16, circum))

    def hold(s):
        neumann = jnp.zeros((16, 128), f32)
        picked = None
        for part in split(mot[s].reshape(axial * 16, circum)):
            term = dot(part, onehot[...], ((1,), (0,)))
            picked = term if picked is None else picked + term
        picked = picked.reshape(axial, 16, 128)
        for r in range(axial):
            neumann = neumann + picked[r] * rowhot[r : r + 1]
        held[...] = 0.5 * dens[...] + neumann

    radial = jnp.sqrt(own[0:1] * own[0:1] + own[1:2] * own[1:2])
    eye = lax.broadcasted_iota(jnp.int32, (pd, 128), 0) == lax.broadcasted_iota(
        jnp.int32, (pd, 128), 1
    )

    def column(line):
        return jnp.sum(jnp.where(eye, jnp.broadcast_to(line, (pd, 128)), 0.0), axis=1, keepdims=True)

    tx, ty, tz = column(own[0:1]), column(own[1:2]), column(own[2:3])
    nx, ny = column(own[0:1] / radial), column(own[1:2] / radial)
    weight_row = own[3:4] * (pd * nb * nc / (8.0 * math.pi))

    hold(0)
    pb_all.wait_recv()

    per = mats.shape[2] // 128
    for q in range(nb // per):
        for i in range(per):
            src = pb[q * per + i]
            dx, dy, dz = tx - src[0:1], ty - src[1:2], tz - src[2:3]
            area = src[3:4]
            dist_sq = dx * dx + dy * dy + dz * dz + area * (1.0 / math.pi)
            inverse = lax.rsqrt(dist_sq)
            phase = (wave_number * dist_sq) * inverse
            turns = phase * (1.0 / (2.0 * math.pi))
            turns = turns - jnp.round(turns)
            sq = turns * turns
            cosine = poly(COS, sq)
            sine = poly(SIN, sq) * turns
            weight = area * (1.0 / (4.0 * math.pi)) * inverse
            single = single_scale * weight
            double = double_scale * weight * (nx * dx + ny * dy) * inverse * inverse
            at = pl.ds(i * 128, 128)
            bf = jnp.bfloat16
            mats[q, 0:pd, at] = (single * cosine).astype(bf)
            mats[q, pd : 2 * pd, at] = (double * (-cosine - phase * sine)).astype(bf)
            mats[q, 2 * pd : 3 * pd, at] = (single * sine).astype(bf)
            mats[q, 3 * pd : 4 * pd, at] = (double * (phase * cosine - sine)).astype(bf)

    left_lanes = (lane & 3) >= 2

    def sweep(s):
        tile = lambda d: cols_in[s, d - 2].astype(f32)
        width = circum + 128
        v, moment, out = {}, {}, {}

        def across(x):
            return pltpu.roll(x, 1, 1) + pltpu.roll(x, width - 1, 1) - 4.0 * x

        def bending(r, lap):
            moment[r] = kext[r + 1, :, : lap.shape[1]] * lap

        def update(r):
            bend = (
                across(moment[r])[:, :circum]
                + moment[r - 1][:, :circum]
                + moment[r + 1][:, :circum]
            )
            here, load = mot[s, r], frc[axial + r]
            bend_re, bend_im = bend[:8], bend[8:]
            v_re, v_im = here[:8], here[8:]
            sh, a, m = coef[0, r], coef[1, r], coef[2, r]
            res_re = load[:8] - (bend_re - loss_factor * bend_im + sh * v_re)
            res_im = load[8:] - (bend_im + loss_factor * bend_re + sh * v_im)
            new = jnp.concatenate(
                [v_re + res_re * a + res_im * m, v_im + res_im * a - res_re * m], axis=0
            )
            mot[s + 1, r] = new
            out[r] = new

        shell_recv(s, LEFT).wait_recv()
        shell_recv(s, RIGHT).wait_recv()
        side_own = jnp.where(left_lanes, tile(LEFT), tile(RIGHT))
        for r in range(axial):
            edge = pltpu.roll(side_own, 4 * r, 1) if r else side_own
            v[r] = jnp.concatenate([mot[s, r], edge], axis=1)
        for r in range(1, axial - 1):
            bending(r, across(v[r]) + v[r - 1] + v[r + 1])
        for r in range(2, axial - 2):
            update(r)

        for_far(lambda d: shell_recv(s, d).wait_recv())
        side_up = jnp.where(left_lanes, tile(UL), tile(UR))
        side_down = jnp.where(left_lanes, tile(DL), tile(DR))
        above = [rows_in[s, 0, i].astype(f32) for i in range(2)]
        below = [rows_in[s, 1, i].astype(f32) for i in range(2)]
        v[-1] = jnp.concatenate([above[1], pltpu.roll(side_up, 4 * (axial - 1), 1)], axis=1)
        v[axial] = jnp.concatenate([below[0], side_down], axis=1)
        bending(-1, across(v[-1])[:, :circum] + above[0] + v[0][:, :circum])
        bending(axial, across(v[axial])[:, :circum] + below[1] + v[axial - 1][:, :circum])
        for r in (0, axial - 1):
            bending(r, across(v[r]) + v[r - 1] + v[r + 1])
        for r in (0, 1, axial - 2, axial - 1):
            update(r)
        return [out[r] for r in range(axial)]

    def round_body(rnd, _):
        b_all(rnd).wait_recv()
        total = None
        for q in range(nb // per):
            block = jnp.concatenate([gb[rnd, q * per + i] for i in range(per)], axis=1)
            term = dot(block, mats[q], ((1,), (1,)))
            total = term if total is None else total + term
        re, im = total[:8], total[8:]
        both = jnp.concatenate(
            [re - pltpu.roll(im, 2 * pd, 1), im + pltpu.roll(re, 2 * pd, 1)], axis=0
        )
        pressure = spread(both)
        press[...] = pressure
        double = spread(pltpu.roll(both, 128 - pd, 1))
        s = SWEEPS * rnd
        density = held[...] - double
        dens[...] = density

        @pl.when(rnd < ITERS - 1)
        def _():
            ga_src[rnd + 1] = density.astype(jnp.bfloat16)
            a_start(rnd + 1)

        weighted = jnp.where(lane < pd, pressure * weight_row, 0.0)
        spots = jnp.concatenate([weighted * rowhot[r : r + 1] for r in range(axial)], axis=0)
        fluid = None
        for part in split(spots):
            term = dot(part, onehot[...], ((1,), (1,)))
            fluid = term if fluid is None else fluid + term
        fluid = fluid.reshape(axial, 16, circum)
        for r in range(axial):
            frc[axial + r] = frc[r] - fluid[r]

        for i in range(SWEEPS):
            rows = sweep(s + i)
            if i < SWEEPS - 1:
                shell_start(s + i + 1, rows)

                @pl.when(rnd < ITERS - 1)
                def _():
                    a_wait(rnd + 1)
                    b_start(rnd + 1)
            else:
                @pl.when(rnd < ITERS - 1)
                def _():
                    shell_start(s + i + 1, rows)
                    hold(s + i + 1)
        return 0

    lax.fori_loop(0, ITERS, round_body, 0)

    density_out[...] = dens[...][:, :pd]
    pressure_out[...] = press[...][:, :pd]
    for r in range(axial):
        motion_out[:, r, :] = mot[STEPS, r]

    for j in range(1, nc):
        copy(pa_src, pa.at[j - 1], pan_send.at[j - 1], pan_recv.at[j - 1], me).wait_send()
    pb_all.wait_send()
    for_dirs(lambda d: stiff_copy(d).wait_send() if d in stiff_dirs else None)

    def finish_round(rnd, _):
        for j in range(1, nc):
            copy(ga_src.at[rnd], ga.at[rnd, j - 1], a_send.at[rnd, j - 1], a_recv.at[rnd, j - 1],
                 me).wait_send()
        b_all(rnd).wait_send()
        for i in range(SWEEPS):
            for_dirs(lambda d: shell_copy(SWEEPS * rnd + i, d).wait_send())
        return 0

    lax.fori_loop(0, ITERS, finish_round, 0)


def per_device(nb, nc, panels, node, hoops, density, motion, force, stiffness):
    pd = panels.shape[1]
    channels, axial, circum = motion.shape
    per = math.gcd(nb, 8)
    f32, bf16 = jnp.float32, jnp.bfloat16
    vmem = pl.BlockSpec(memory_space=pltpu.VMEM)
    hbm = pl.BlockSpec(memory_space=pltpu.HBM)
    dma = pltpu.SemaphoreType.DMA
    scratch = [
        pltpu.VMEM((STEPS + 1, axial, channels, circum), f32),
        pltpu.VMEM((2 * axial, channels, circum), f32),
        pltpu.VMEM((STEPS, 2, 2, channels, circum), bf16),
        pltpu.VMEM((STEPS, 2, 2, channels, circum), bf16),
        pltpu.VMEM((STEPS, 6, channels, 128), bf16),
        pltpu.VMEM((STEPS, channels, 128), bf16),
        pltpu.VMEM((4, axial, circum), f32),
        pltpu.VMEM((axial + 2, channels, circum + 128), f32),
        pltpu.VMEM((3, axial, 8, circum), f32),
        pltpu.VMEM((circum, 128), bf16),
        pltpu.VMEM((8, 128), f32),
        pltpu.VMEM((channels, 128), f32),
        pltpu.VMEM((channels, 128), f32),
        pltpu.VMEM((channels, 128), f32),
        pltpu.VMEM((24, 128), f32),
        pltpu.VMEM((ITERS, nc - 1, channels, 128), bf16),
        pltpu.VMEM((ITERS, nb, channels, 128), bf16),
        pltpu.VMEM((ITERS, channels, 128), bf16),
        pltpu.VMEM((nc - 1, 8, 128), f32),
        pltpu.VMEM((nb, 8, 128), f32),
        pltpu.VMEM((8, 128), f32),
        pltpu.VMEM((nb // per, 4 * pd, per * 128), bf16),
        dma((STEPS, 8)), dma((STEPS, 8)), dma((4,)), dma((4,)),
        dma((ITERS, nc - 1)), dma((ITERS, nc - 1)), dma((ITERS,)), dma((ITERS,)),
        dma((nc,)), dma((nc,)),
        pltpu.VMEM(panels.shape, f32), pltpu.SMEM(node.shape, jnp.int32),
        pltpu.SMEM(hoops.shape, jnp.int32), pltpu.VMEM(density.shape, f32),
        pltpu.VMEM(motion.shape, f32), pltpu.VMEM(force.shape, f32),
        pltpu.VMEM(stiffness.shape, f32), dma((7,)),
    ]
    return pl.pallas_call(
        functools.partial(kernel, nb, nc, pd),
        out_shape=(
            jax.ShapeDtypeStruct(density.shape, f32),
            jax.ShapeDtypeStruct(density.shape, f32),
            jax.ShapeDtypeStruct(motion.shape, f32),
        ),
        in_specs=[hbm] * 7,
        out_specs=(vmem, vmem, vmem),
        scratch_shapes=scratch,
        compiler_params=pltpu.CompilerParams(
            collective_id=0, has_side_effects=True, vmem_limit_bytes=64 * 1024 * 1024
        ),
    )(panels, node, hoops, density, motion, force, stiffness)


def solution(mesh):
    nb, nc = mesh.shape["blk"], mesh.shape["circ"]
    in_specs = (
        P(None, ("blk", "circ")),
        P(("blk", "circ")),
        P(),
        P(None, ("blk", "circ")),
        P(None, "blk", "circ"),
        P(None, "blk", "circ"),
        P("blk", "circ"),
    )
    out_specs = (P(None, ("blk", "circ")), P(None, ("blk", "circ")), P(None, "blk", "circ"))
    return jax.shard_map(
        functools.partial(per_device, nb, nc),
        mesh=mesh, in_specs=in_specs, out_specs=out_specs, check_vma=False,
    )
```
